256 devices in a mesh: dp: 32 (over z_lo, x, core), tp: 8 (over z_hi, y).
Axes of the slice: x: 4, y: 4, z: 8 (z_hi: 2, z_lo: 4; z = z_hi * 4 + z_lo), core: 2. Of those that a mesh axis runs over, the one named last changes fastest.
Arguments:
- tokens: bfloat16 [6144, 3584], P('dp', 'tp'), may hold values from -6 to 6
- cotangent: bfloat16 [6144, 3584], P('dp', 'tp'), may hold values from -6 to 6
- working: bfloat16 [32, 8, 3, 384, 3584], P('dp', 'tp'), may hold values from -0.09375 to 0.09375
- degraded: int32 [32], P('dp'), may hold values from 0 to 1, as said below
- block_map: int32 [32, 16], P('dp'), may hold values from 0 to 7, as said below
- master: float32 [3, 2048, 3584], P(None, ('tp', 'dp')), may hold values from -6 to 6
- moment_one: float32 [3, 2048, 3584], P(None, ('tp', 'dp')), may hold values from -6 to 6
- moment_two: float32 [3, 2048, 3584], P(None, ('tp', 'dp')), may hold values from 0.5 to 8
Outputs:
- input_grad: bfloat16 [6144, 3584], P('dp', 'tp')
- master_next: float32 [3, 2048, 3584], P(None, ('tp', 'dp'))
- moment_one_next: float32 [3, 2048, 3584], P(None, ('tp', 'dp'))
- moment_two_next: float32 [3, 2048, 3584], P(None, ('tp', 'dp'))
The draws below stay inside these ranges and needn't reach their ends.
Inputs may be any that keep to these rules, and one draw needn't show every extreme that they name: `degraded`: exactly 8 replicas have the value 1. `block_map`: in every row the 16 blocks lie on 6 distinct devices, each of which holds 2 or 3 of them, and at least one holds 3. A row is read only where degraded is 1.
All inputs are finite; a program needn't handle non-finite values.
Results may differ from the reference program's by a relative error of at most 0.0075.
Values may be sent and summed in bfloat16 or wider, within the bound.
A program may use at most 64 MiB of HBM per device.

```python
import math
import jax
import jax.numpy as jnp
from jax import lax

D = 3584
BLOCK = 128
BLOCKS = 16
FF = 2048
TOK = 192
TOKENS = 6144
USED = 6
SLOTS = 3
N_DP = 32
N_TP = 8


def draw_degraded(key, part):
    shuffled = jax.random.permutation(key, N_DP).astype(jnp.int32)
    return (shuffled < N_DP // 4).astype(jnp.int32)


def draw_block_map(key, part):

    def one_row(row_index):
        row_key = jax.random.fold_in(key, row_index)
        devices = jax.random.permutation(jax.random.fold_in(row_key, 1), N_TP).astype(jnp.int32)
        block_order = jax.random.permutation(jax.random.fold_in(row_key, 2), BLOCKS).astype(jnp.int32)
        holder = devices[jnp.arange(BLOCKS, dtype=jnp.int32) % USED]
        return jnp.zeros((BLOCKS,), jnp.int32).at[block_order].set(holder)
    return jax.vmap(one_row)(jnp.arange(N_DP, dtype=jnp.int32))


def levels(key, extent, shards, least, high):
    def one(axis_at, blocks):
        heights = jax.random.uniform(jax.random.fold_in(jax.random.fold_in(key, 6), axis_at), (blocks,), jnp.float32, least / len(shards), high / len(shards))
        return jnp.repeat(jnp.exp(heights), extent[axis_at] // blocks).reshape((-1,) + (1,) * (len(extent) - axis_at - 1))

    level = one(*shards[0])
    for cut in shards[1:]:
        level = level * one(*cut)
    return level


def scatter_about(rng, shape, scale, reach, shards=(), kind=jnp.bfloat16):
    entries = scale * jax.random.normal(rng, shape, jnp.float32)
    if shards:
        entries = entries * levels(rng, shape, shards, -0.22, 0.18)
    return jnp.clip(entries, -reach, reach).astype(kind)


def setup_inputs(seed: int = 0) -> dict:
    splits = jax.random.split(jax.random.key(seed), 9)
    tokens = scatter_about(splits[0], (TOKENS, D), 1.0, 6.0, ((0, 32), (1, 8)))
    cotangent = scatter_about(splits[1], (TOKENS, D), 1.0, 6.0, ((0, 32), (1, 8)))
    working = scatter_about(splits[2], (N_DP, N_TP, 3, SLOTS * BLOCK, D), D ** -0.5, 0.09375, ((0, 32), (1, 8)))
    degraded = draw_degraded(jax.random.fold_in(splits[8], 71), 0)
    block_map = draw_block_map(jax.random.fold_in(splits[8], 71), 0)
    master = scatter_about(splits[5], (3, FF, D), 1.0, 6.0, ((1, 256),), jnp.float32)
    moment_one = scatter_about(splits[6], (3, FF, D), 1.0, 6.0, ((1, 256),), jnp.float32)
    moment_two = jnp.clip(jnp.exp(math.log(8.0) - 2.7725887 * jax.random.uniform(splits[7], (3, FF, D), jnp.float32) ** levels(splits[7], (3, FF, D), ((1, 256),), -0.2, 0.2)), 0.5, 8.0)
    return dict(tokens=tokens, cotangent=cotangent, working=working, degraded=degraded, block_map=block_map, master=master, moment_one=moment_one, moment_two=moment_two)


beta_one = 0.9
beta_two = 0.95
learn_rate = 0.05
decay_rate = 0.1
adam_eps = 1e-08
bias_one = 1.0 - 0.9 ** 10
bias_two = 1.0 - 0.95 ** 10

def layout_places(replica_flag, mapping):
    blocks = jnp.arange(BLOCKS, dtype=jnp.int32)
    canonical = (blocks // (BLOCKS // N_TP)).astype(jnp.int32)
    holder = jnp.where(replica_flag > 0, mapping, canonical).astype(jnp.int32)
    earlier = (holder[None, :] == holder[:, None]) & (blocks[None, :] < blocks[:, None])
    slot_rank = lax.optimization_barrier(jnp.sum(earlier.astype(jnp.int32), axis=1)).astype(jnp.int32)
    return (holder * SLOTS + slot_rank).astype(jnp.int32)

def replica_step(running, items):
    tok_rep, cot_rep, work_rep, replica_flag, mapping = items
    places = layout_places(replica_flag, mapping)
    stacked = work_rep.reshape(N_TP, 3, SLOTS, BLOCK, D).transpose(0, 2, 1, 3, 4).reshape(N_TP * SLOTS, 3, BLOCK, D)
    chosen = jnp.take(stacked, places, axis=0)
    weights = chosen.transpose(1, 0, 2, 3).reshape(3, FF, D)
    contract_d = (((1,), (1,)), ((), ()))
    gate_pre = lax.dot_general(tok_rep, weights[0], contract_d, preferred_element_type=jnp.float32)
    up_pre = lax.dot_general(tok_rep, weights[1], contract_d, preferred_element_type=jnp.float32)
    hidden_grad = lax.dot_general(cot_rep, weights[2], contract_d, preferred_element_type=jnp.float32)
    gate_sig = jax.nn.sigmoid(gate_pre)
    active = gate_pre * gate_sig
    hidden = (active * up_pre).astype(jnp.bfloat16)
    gate_grad = (hidden_grad * up_pre * gate_sig * (1.0 + gate_pre * (1.0 - gate_sig))).astype(jnp.bfloat16)
    up_grad = (hidden_grad * active).astype(jnp.bfloat16)
    input_rep = (jnp.dot(gate_grad, weights[0], preferred_element_type=jnp.float32) + jnp.dot(up_grad, weights[1], preferred_element_type=jnp.float32)).astype(jnp.bfloat16)
    contract_t = (((0,), (0,)), ((), ()))
    gate_term = lax.dot_general(gate_grad, tok_rep, contract_t, preferred_element_type=jnp.float32)
    up_term = lax.dot_general(up_grad, tok_rep, contract_t, preferred_element_type=jnp.float32)
    down_term = lax.dot_general(hidden, cot_rep, contract_t, preferred_element_type=jnp.float32)
    return (running + jnp.stack([gate_term, up_term, down_term], axis=0), input_rep)

def reference(tokens, cotangent, working, degraded, block_map, master, moment_one, moment_two):
    items = (tokens.reshape(N_DP, TOK, D), cotangent.reshape(N_DP, TOK, D), working, degraded, block_map)
    initial = jnp.zeros((3, FF, D), jnp.float32)
    summed, inputs_all = lax.scan(replica_step, initial, items)
    grad_mean = summed / N_DP
    moment_one_next = beta_one * moment_one + (1.0 - beta_one) * grad_mean
    moment_two_next = beta_two * moment_two + (1.0 - beta_two) * grad_mean * grad_mean
    update = moment_one_next / bias_one / (jnp.sqrt(moment_two_next / bias_two) + adam_eps) + decay_rate * master
    master_next = master - learn_rate * update
    return (inputs_all.reshape(TOKENS, D), master_next, moment_one_next, moment_two_next)
```

```python
import jax
import jax.numpy as jnp
from jax import lax
from jax.experimental import pallas as pl
from jax.experimental.pallas import tpu as pltpu
from jax.sharding import PartitionSpec as P

MESH = pl.DeviceIdType.MESH
F32, BF16 = jnp.float32, jnp.bfloat16

D = 3584
BLOCK = 128
BLOCKS = 16
SLOTS = 3
TOK = 192
N_Y, N_ZH, N_X, N_ZL = 4, 2, 4, 4
N_TP = N_Y * N_ZH
REPLICAS = N_X * N_ZL * 2
SHARD = D // N_TP
HALF = D // 2
COLS = 256
CHUNKS = HALF // COLS
ROWS = 16

beta_one = 0.9
beta_two = 0.95
learn_rate = 0.05
decay_rate = 0.1
adam_eps = 1e-08
bias_one = 1.0 - 0.9**10
bias_two = 1.0 - 0.95**10

NT = (((1,), (1,)), ((), ()))


def kernel(
    tok, cot, work, flag, bmap, master, mom_one, mom_two,
    ig_out, master_out, one_out, two_out,
    w, state, land, xfull, gfull, xo, go,
    mask, fill, acts, contrib, act_land, act_zsend, act_zland, fin, fin_o, lhs, lhs_o,
    ig_send, ig_land, ig_zsend, ig_zland, ig_own,
    g_send, x_land, x_sum, z_send, z_land, c_own, c_land,
    w_sem, state_sem, p1_s, p1_r, cx_s, cx_r,
    act_s, act_r, az_s, az_r, ac_s, ac_r,
    ig_s, ig_r, iz_s, iz_r,
    x_s, x_r, z_s, z_r, c_s, c_r,
):
    dp, tp = lax.axis_index("dp"), lax.axis_index("tp")
    zl, x, c = lax.div(dp, 8), lax.rem(lax.div(dp, 2), 4), lax.rem(dp, 2)
    zh, y = lax.div(tp, 4), lax.rem(tp, 4)
    oh = 1 - zh

    def at(zh_, y_):
        return zh_ * 4 + y_

    def y_dev(j):
        return (dp, at(zh, lax.rem(y + j, 4)))

    def x_dev(j):
        return (zl * 8 + lax.rem(x + j, 4) * 2 + c, tp)

    def z_dev(j):
        return (lax.rem(zl + j, 4) * 8 + x * 2 + c, tp)

    anti = at(oh, y)
    anti_dev = (dp, anti)
    core_dev = (zl * 8 + x * 2 + (1 - c), tp)

    def remote(src, dst, ssem, rsem, dev):
        return pltpu.make_async_remote_copy(
            src_ref=src, dst_ref=dst, send_sem=ssem, recv_sem=rsem, device_id=dev, device_id_type=MESH
        )

    barrier = pltpu.get_barrier_semaphore()
    for dev in [y_dev(1), y_dev(2), y_dev(3), anti_dev, core_dev, x_dev(1), x_dev(2), x_dev(3), z_dev(1), z_dev(2), z_dev(3)]:
        pl.semaphore_signal(barrier, inc=1, device_id=dev, device_id_type=MESH)

    w_copies = [pltpu.make_async_copy(work.at[k], w.at[k], w_sem.at[k]) for k in range(3)]
    for cp in w_copies:
        cp.start()
    state_copies = [
        pltpu.make_async_copy(ref, state.at[i], state_sem.at[i]) for i, ref in enumerate((master, mom_one, mom_two))
    ]
    for cp in state_copies:
        cp.start()
    land[tp, 0] = tok[...]
    land[tp, 1] = cot[...]

    count = jnp.int32(0)
    filled = [jnp.float32(0.0)] * SLOTS
    for b in range(BLOCKS):
        holder = jnp.where(flag[0] > 0, bmap[0, b], b // 2)
        mine = jnp.where(holder == tp, 1, 0)
        for s in range(SLOTS):
            hit = (mine * jnp.where(count == s, 1, 0)).astype(F32)
            mask[b * SLOTS + s] = hit
            filled[s] = filled[s] + hit
        count = count + mine
    for s in range(SLOTS):
        fill[s] = filled[s]

    pl.semaphore_wait(barrier, 11)

    right, left = y_dev(1), y_dev(3)
    yr, yl = lax.rem(y + 1, 4), lax.rem(y + 3, 4)
    p1 = {}

    def send(index, chunk, a, dev):
        cp = remote(land.at[chunk, a], land.at[chunk, a], p1_s.at[index], p1_r.at[index], dev)
        cp.start()
        p1[index] = cp

    send(0, tp, 0, anti_dev)
    send(2, tp, 0, right)
    send(5, tp, 1, left)
    send(1, tp, 1, anti_dev)
    send(3, tp, 1, right)
    send(4, tp, 0, left)
    p1[2].wait_recv()
    send(6, at(zh, yl), 0, right)
    p1[5].wait_recv()
    send(7, at(zh, yr), 1, left)
    p1[0].wait_recv()
    send(8, anti, 0, right)
    send(10, anti, 0, left)
    p1[1].wait_recv()
    send(11, anti, 1, left)
    send(9, anti, 1, right)
    p1[8].wait_recv()
    send(12, at(oh, yl), 0, right)
    p1[11].wait_recv()
    send(13, at(oh, yr), 1, left)
    for index in (3, 4, 6, 7, 9, 10, 12, 13):
        p1[index].wait_recv()

    for j in range(N_TP):
        xfull[:, j * SHARD : (j + 1) * SHARD] = land[j, 0]
        gfull[:, j * SHARD : (j + 1) * SHARD] = land[j, 1]

    other_cols = pl.ds(pl.multiple_of((1 - c) * HALF, HALF), HALF)
    cx = [
        remote(xfull.at[:, other_cols], xo, cx_s.at[0], cx_r.at[0], core_dev),
        remote(gfull.at[:, other_cols], go, cx_s.at[1], cx_r.at[1], core_dev),
    ]
    for cp in cx:
        cp.start()

    for cp in w_copies:
        cp.wait()
    zg = lax.dot_general(xfull[...], w[0], NT, preferred_element_type=F32)
    zu = lax.dot_general(xfull[...], w[1], NT, preferred_element_type=F32)
    dh = lax.dot_general(gfull[...], w[2], NT, preferred_element_type=F32)
    sig = jax.nn.sigmoid(zg)
    active = zg * sig
    kinds = (
        (dh * zu * sig * (1.0 + zg * (1.0 - sig))).astype(BF16),
        (dh * active).astype(BF16),
        (active * zu).astype(BF16),
    )
    for k in range(3):
        for s in range(SLOTS):
            acts[s, k] = kinds[k][:, s * BLOCK : (s + 1) * BLOCK]

    def contribute(owner):
        for i in range(2):
            base = (owner * 2 + i) * SLOTS
            m = [jnp.full((TOK, BLOCK), mask[base + s], F32).astype(BF16) for s in range(SLOTS)]
            for k in range(3):
                contrib[owner, i * 3 + k] = acts[0, k] * m[0] + acts[1, k] * m[1] + acts[2, k] * m[2]

    act = {}
    for part, zt in ((0, oh), (1, zh)):
        for j in (2, 1, 3):
            owner = at(zt, lax.rem(y + j, 4))
            contribute(owner)
            cp = remote(
                contrib.at[owner], act_land.at[j - 1, part], act_s.at[j - 1, part], act_r.at[j - 1, part], y_dev(j)
            )
            cp.start()
            act[j, part] = cp
    contribute(anti)
    contribute(tp)

    gate_m = jnp.concatenate(
        [acts[s, 0] * jnp.full((TOK, BLOCK), fill[s], F32).astype(BF16) for s in range(SLOTS)], axis=1
    )
    up_m = jnp.concatenate(
        [acts[s, 1] * jnp.full((TOK, BLOCK), fill[s], F32).astype(BF16) for s in range(SLOTS)], axis=1
    )
    for p in range(N_TP // 2):
        cols = slice(p * 2 * SHARD, (p + 1) * 2 * SHARD)
        value = (
            jnp.dot(gate_m, w[0, :, cols], preferred_element_type=F32)
            + jnp.dot(up_m, w[1, :, cols], preferred_element_type=F32)
        ).astype(BF16)
        ig_send[2 * p] = value[:, :SHARD]
        ig_send[2 * p + 1] = value[:, SHARD:]

    for j in (2, 1, 3):
        act[j, 0].wait_recv()
    for i in range(6):
        act_zsend[i] = (contrib[anti, i] + act_land[0, 0, i]) + (act_land[1, 0, i] + act_land[2, 0, i])
    az = remote(act_zsend, act_zland, az_s, az_r, anti_dev)
    az.start()
    for j in (2, 1, 3):
        act[j, 1].wait_recv()

    ig = {}
    for part, zt in ((0, oh), (1, zh)):
        for j in (2, 1, 3):
            owner = at(zt, lax.rem(y + j, 4))
            cp = remote(
                ig_send.at[owner], ig_land.at[j - 1, part], ig_s.at[j - 1, part], ig_r.at[j - 1, part], y_dev(j)
            )
            cp.start()
            ig[j, part] = cp

    for i in range(6):
        fin[i] = (contrib[tp, i] + act_land[0, 1, i]) + (act_land[1, 1, i] + act_land[2, 1, i])
    az.wait_recv()
    for i in range(6):
        fin[i] = fin[i] + act_zland[i]
    ac = remote(fin, fin_o, ac_s, ac_r, core_dev)
    ac.start()
    for k in range(3):
        for i in range(2):
            lhs[k, i * BLOCK : (i + 1) * BLOCK, :] = fin[i * 3 + k].T
    for cp in cx:
        cp.wait_recv()
    ac.wait_recv()
    for k in range(3):
        for i in range(2):
            lhs_o[k, i * BLOCK : (i + 1) * BLOCK, :] = fin_o[i * 3 + k].T

    def x_copy(n, j):
        return remote(
            g_send.at[n, lax.rem(x + j, 4)], x_land.at[n, j - 1], x_s.at[n, j - 1], x_r.at[n, j - 1], x_dev(j)
        )

    def z_copy(n, j):
        return remote(
            z_send.at[n, lax.rem(zl + j, 4)], z_land.at[n, j - 1], z_s.at[n, j - 1], z_r.at[n, j - 1], z_dev(j)
        )

    @pl.loop(0, CHUNKS)
    def _(n):
        mine = pl.ds(pl.multiple_of(c * HALF + n * COLS, COLS), COLS)
        cols = pl.ds(pl.multiple_of(n * COLS, COLS), COLS)
        for k in range(3):
            own, other = (xfull, xo) if k < 2 else (gfull, go)
            value = (
                jnp.dot(lhs[k], own[:, mine], preferred_element_type=F32)
                + jnp.dot(lhs_o[k], other[:, cols], preferred_element_type=F32)
            ).astype(BF16)
            for zt in range(N_ZL):
                for xt in range(N_X):
                    row = (zt * N_X + xt) * ROWS
                    g_send[n, xt, zt, k] = value[row : row + ROWS]
        for j in (2, 1, 3):
            x_copy(n, j).start()

    for j in (2, 1, 3):
        ig[j, 0].wait_recv()
    ig_zsend[...] = (
        (ig_send[anti].astype(F32) + ig_land[0, 0].astype(F32))
        + (ig_land[1, 0].astype(F32) + ig_land[2, 0].astype(F32))
    ).astype(BF16)
    iz = remote(ig_zsend, ig_zland, iz_s, iz_r, anti_dev)
    iz.start()
    for j in (2, 1, 3):
        ig[j, 1].wait_recv()
    ig_own[...] = (ig_send[tp].astype(F32) + ig_land[0, 1].astype(F32)) + (
        ig_land[1, 1].astype(F32) + ig_land[2, 1].astype(F32)
    )

    @pl.loop(0, CHUNKS)
    def _(n):
        for j in (1, 3, 2):
            x_copy(n, j).wait_recv()
        for zt in range(N_ZL):
            for k in range(3):
                value = (g_send[n, x, zt, k].astype(F32) + x_land[n, 0, zt, k].astype(F32)) + (
                    x_land[n, 1, zt, k].astype(F32) + x_land[n, 2, zt, k].astype(F32)
                )
                x_sum[n, zt, k] = value
                z_send[n, zt, k] = value.astype(BF16)
        for j in (3, 2, 1):
            z_copy(n, j).start()

    iz.wait_recv()
    ig_out[...] = (ig_own[...] + ig_zland[...].astype(F32)).astype(BF16)

    @pl.loop(0, CHUNKS)
    def _(n):
        cols = pl.ds(pl.multiple_of(n * COLS, COLS), COLS)
        for j in (1, 2, 3):
            z_copy(n, j).wait_recv()
        for k in range(3):
            value = (x_sum[n, zl, k] + z_land[n, 0, k].astype(F32)) + (
                z_land[n, 1, k].astype(F32) + z_land[n, 2, k].astype(F32)
            )
            c_own[0, k, :, cols] = value[:8]
            c_own[1, k, :, cols] = value[8:]

    cc = remote(c_own.at[1 - c], c_land, c_s, c_r, core_dev)
    cc.start()
    for cp in state_copies:
        cp.wait()

    def adam(read, start):
        cols = pl.ds(pl.multiple_of(start, HALF), HALF)
        for k in range(3):
            grad = read(k) * (1.0 / REPLICAS)
            one = beta_one * state[1, k, :, cols] + (1.0 - beta_one) * grad
            two = beta_two * state[2, k, :, cols] + (1.0 - beta_two) * grad * grad
            old = state[0, k, :, cols]
            update = one / bias_one / (jnp.sqrt(two / bias_two) + adam_eps) + decay_rate * old
            master_out[k, :, cols] = old - learn_rate * update
            one_out[k, :, cols] = one
            two_out[k, :, cols] = two

    adam(lambda k: c_own[c, k], c * HALF)
    cc.wait_recv()
    adam(lambda k: c_land[k], (1 - c) * HALF)

    for cp in p1.values():
        cp.wait_send()
    for cp in cx + list(act.values()) + [az, ac] + list(ig.values()) + [iz, cc]:
        cp.wait_send()

    @pl.loop(0, CHUNKS)
    def _(n):
        for j in (1, 2, 3):
            x_copy(n, j).wait_send()
            z_copy(n, j).wait_send()


def per_device(tokens, cotangent, working, degraded, block_map, master, moment_one, moment_two):
    vmem = pl.BlockSpec(memory_space=pltpu.VMEM)
    smem = pl.BlockSpec(memory_space=pltpu.SMEM)
    hbm = pl.BlockSpec(memory_space=pl.ANY)
    dma = pltpu.SemaphoreType.DMA
    rows = (3, 8, D)
    return pl.pallas_call(
        kernel,
        name="swiglu_step",
        out_shape=(
            jax.ShapeDtypeStruct((TOK, SHARD), BF16),
            jax.ShapeDtypeStruct(rows, F32),
            jax.ShapeDtypeStruct(rows, F32),
            jax.ShapeDtypeStruct(rows, F32),
        ),
        in_specs=[vmem, vmem, hbm, smem, smem, hbm, hbm, hbm],
        out_specs=(vmem,) * 4,
        scratch_shapes=[
            pltpu.VMEM((3, SLOTS * BLOCK, D), BF16),
            pltpu.VMEM((3,) + rows, F32),
            pltpu.VMEM((N_TP, 2, TOK, SHARD), BF16),
            pltpu.VMEM((TOK, D), BF16),
            pltpu.VMEM((TOK, D), BF16),
            pltpu.VMEM((TOK, HALF), BF16),
            pltpu.VMEM((TOK, HALF), BF16),
            pltpu.SMEM((BLOCKS * SLOTS,), F32),
            pltpu.SMEM((SLOTS,), F32),
            pltpu.VMEM((SLOTS, 3, TOK, BLOCK), BF16),
            pltpu.VMEM((N_TP, 6, TOK, BLOCK), BF16),
            pltpu.VMEM((3, 2, 6, TOK, BLOCK), BF16),
            pltpu.VMEM((6, TOK, BLOCK), BF16),
            pltpu.VMEM((6, TOK, BLOCK), BF16),
            pltpu.VMEM((6, TOK, BLOCK), BF16),
            pltpu.VMEM((6, TOK, BLOCK), BF16),
            pltpu.VMEM((3, 2 * BLOCK, TOK), BF16),
            pltpu.VMEM((3, 2 * BLOCK, TOK), BF16),
            pltpu.VMEM((N_TP, TOK, SHARD), BF16),
            pltpu.VMEM((3, 2, TOK, SHARD), BF16),
            pltpu.VMEM((TOK, SHARD), BF16),
            pltpu.VMEM((TOK, SHARD), BF16),
            pltpu.VMEM((TOK, SHARD), F32),
            pltpu.VMEM((CHUNKS, N_X, N_ZL, 3, ROWS, COLS), BF16),
            pltpu.VMEM((CHUNKS, 3, N_ZL, 3, ROWS, COLS), BF16),
            pltpu.VMEM((CHUNKS, N_ZL, 3, ROWS, COLS), F32),
            pltpu.VMEM((CHUNKS, N_ZL, 3, ROWS, COLS), BF16),
            pltpu.VMEM((CHUNKS, 3, 3, ROWS, COLS), BF16),
            pltpu.VMEM((2, 3, 8, HALF), F32),
            pltpu.VMEM((3, 8, HALF), F32),
            dma((3,)),
            dma((3,)),
            dma((14,)),
            dma((14,)),
            dma((2,)),
            dma((2,)),
            dma((3, 2)),
            dma((3, 2)),
            dma,
            dma,
            dma,
            dma,
            dma((3, 2)),
            dma((3, 2)),
            dma,
            dma,
            dma((CHUNKS, 3)),
            dma((CHUNKS, 3)),
            dma((CHUNKS, 3)),
            dma((CHUNKS, 3)),
            dma,
            dma,
        ],
        compiler_params=pltpu.CompilerParams(
            collective_id=0, has_side_effects=True, vmem_limit_bytes=60 * 1024 * 1024
        ),
        cost_estimate=pl.CostEstimate(flops=3_700_000_000, bytes_accessed=12_000_000, transcendentals=73728),
    )(tokens, cotangent, working.reshape(working.shape[2:]), degraded, block_map, master, moment_one, moment_two)


def solution(mesh):
    return jax.shard_map(
        per_device,
        mesh=mesh,
        in_specs=(
            P("dp", "tp"),
            P("dp", "tp"),
            P("dp", "tp", None, None, None),
            P("dp"),
            P("dp", None),
            P(None, ("tp", "dp"), None),
            P(None, ("tp", "dp"), None),
            P(None, ("tp", "dp"), None),
        ),
        out_specs=(
            P("dp", "tp"),
            P(None, ("tp", "dp"), None),
            P(None, ("tp", "dp"), None),
            P(None, ("tp", "dp"), None),
        ),
        check_vma=False,
    )
```

```python
import jax
import jax.numpy as jnp
from jax import lax
from jax.experimental import pallas as pl
from jax.experimental.pallas import tpu as pltpu
from jax.sharding import PartitionSpec as P

MESH = pl.DeviceIdType.MESH
F32, BF16 = jnp.float32, jnp.bfloat16

D = 3584
BLOCK = 128
BLOCKS = 16
SLOTS = 3
TOK = 192
N_Y, N_ZH, N_X, N_ZL = 4, 2, 4, 4
N_TP = N_Y * N_ZH
REPLICAS = N_X * N_ZL * 2
SHARD = D // N_TP
GROUP = 2 * N_X
UNIT = SLOTS * TOK
EARLY, LATE = (0, TOK // 2), (TOK // 2, TOK // 2)

beta_one = 0.9
beta_two = 0.95
learn_rate = 0.05
decay_rate = 0.1
adam_eps = 1e-08
bias_one = 1.0 - 0.9**10
bias_two = 1.0 - 0.95**10

NT = (((1,), (1,)), ((), ()))


def kernel(
    tok, cot, work, flag, bmap,
    ig_out, grad_out,
    w, land, xl, xfull, gfull,
    place, fill, ab, own_sel, az_send, az_land, ftb,
    ig_send, ig_land, ig_zsend, ig_zland, ig_own, act_f,
    part, z_send, z_land, tr, gl,
    w_sem, p1_s, p1_r, xs_s, xs_r,
    ya_s, ya_r, az_s, az_r, xa_s, xa_r,
    ig_s, ig_r, iz_s, iz_r,
    z_s, z_r, tr_s, tr_r,
):
    dp, tp = lax.axis_index("dp"), lax.axis_index("tp")
    zl, x, c = lax.div(dp, 8), lax.rem(lax.div(dp, 2), 4), lax.rem(dp, 2)
    zh, y = lax.div(tp, 4), lax.rem(tp, 4)
    oh = 1 - zh
    oc = 1 - c
    me = c * 4 + x
    seat = x * 2 + c

    def at(zh_, y_):
        return zh_ * 4 + y_

    def y_dev(j):
        return (dp, at(zh, lax.rem(y + j, 4)))

    def group_dev(x_, c_):
        return (zl * 8 + x_ * 2 + c_, tp)

    def z_dev(j):
        return (lax.rem(zl + j, 4) * 8 + x * 2 + c, tp)

    def x_at(j):
        return lax.rem(x + j, 4)

    anti = at(oh, y)
    anti_dev = (dp, anti)
    core_dev = group_dev(x, oc)

    def remote(src, dst, ssem, rsem, dev):
        return pltpu.make_async_remote_copy(
            src_ref=src, dst_ref=dst, send_sem=ssem, recv_sem=rsem, device_id=dev, device_id_type=MESH
        )

    sent = []

    def start(src, dst, ssem, rsem, dev):
        cp = remote(src, dst, ssem, rsem, dev)
        cp.start()
        sent.append(cp)
        return cp

    barrier = pltpu.get_barrier_semaphore()
    partners = [y_dev(1), y_dev(2), y_dev(3), anti_dev, core_dev]
    partners += [group_dev(x_at(j), t) for j in (1, 2, 3) for t in (c, oc)]
    partners += [z_dev(1), z_dev(2), z_dev(3)]
    for dev in partners:
        pl.semaphore_signal(barrier, inc=1, device_id=dev, device_id_type=MESH)

    own_copies = [pltpu.make_async_copy(ref, land.at[tp, a], w_sem.at[3 + a]) for a, ref in ((0, tok), (1, cot))]
    for cp in own_copies:
        cp.start()
    w_copies = [pltpu.make_async_copy(work.at[k], w.at[k], w_sem.at[k]) for k in range(3)]
    for cp in w_copies:
        cp.start()

    holders = [jnp.where(flag[0] > 0, bmap[0, b], b // 2) for b in range(BLOCKS)]
    filled = [jnp.float32(0.0)] * SLOTS
    for b in range(BLOCKS):
        rank = jnp.int32(0)
        for e in range(b):
            rank = rank + jnp.where(holders[e] == holders[b], 1, 0)
        spot = holders[b] * SLOTS + rank
        place[b] = spot
        for s in range(SLOTS):
            filled[s] = filled[s] + jnp.where(spot == tp * SLOTS + s, 1.0, 0.0)
    for s in range(SLOTS):
        fill[s] = filled[s]

    for cp in own_copies:
        cp.wait()
    pl.semaphore_wait(barrier, len(partners))

    right, left = y_dev(1), y_dev(3)
    yr, yl = lax.rem(y + 1, 4), lax.rem(y + 3, 4)
    p1 = {}

    def send(a, index, chunk, dev, rows=(0, TOK)):
        ref = land.at[chunk, a, pl.ds(*rows)]
        p1[a, index] = start(ref, ref, p1_s.at[a, index], p1_r.at[a, index], dev)

    def neighbours(a, half):
        chunk = (tp, anti)[half]
        send(a, 1 + 4 * half, chunk, right)
        send(a, 2 + 4 * half, chunk, left)

    def forward(a, half):
        zt = (zh, oh)[half]
        p1[a, 1 + 4 * half].wait_recv()
        send(a, 3 + 4 * half, at(zt, yl), right, EARLY)
        p1[a, 2 + 4 * half].wait_recv()
        send(a, 4 + 4 * half, at(zt, yr), left, LATE)

    def slices(a, half):
        p1[a, 3 + 4 * half].wait_recv()
        p1[a, 4 + 4 * half].wait_recv()
        zt = (zh, oh)[half]
        for j in (2, 1, 3):
            start(
                land.at[at(zt, x_at(j)), a],
                xl.at[me, a],
                xs_s.at[half * 3 + j - 1, a],
                xs_r.at[me, a],
                group_dev(x_at(j), zt),
            )

    def core_slice(a):
        start(land.at[oc * 4 + x, a], xl.at[me, a], xs_s.at[6, a], xs_r.at[me, a], core_dev)

    send(0, 0, tp, anti_dev)
    neighbours(0, 0)
    send(1, 0, tp, anti_dev)
    forward(0, 0)
    neighbours(1, 0)
    p1[0, 0].wait_recv()
    neighbours(0, 1)
    forward(1, 0)
    slices(0, 0)
    forward(0, 1)
    p1[1, 0].wait_recv()
    neighbours(1, 1)
    slices(1, 0)
    slices(0, 1)
    core_slice(0)

    ya = {}

    def y_send(k, value):
        value = value.astype(BF16)
        for s in range(SLOTS):
            ab[y, k, s * TOK : (s + 1) * TOK] = value[:, s * BLOCK : (s + 1) * BLOCK]
        for q, dev in ((0, right), (1, left)):
            ya[k, q] = start(ab.at[y, k], ab.at[y, k], ya_s.at[k, q], ya_r.at[k, q], dev)

    lower, upper = pl.ds(0, UNIT // 2), pl.ds(UNIT // 2, UNIT // 2)

    def y_forward(k):
        ya[k, 0].wait_recv()
        ya[k, 2] = start(ab.at[yl, k, lower], ab.at[yl, k, lower], ya_s.at[k, 2], ya_r.at[k, 2], right)
        ya[k, 1].wait_recv()
        ya[k, 3] = start(ab.at[yr, k, upper], ab.at[yr, k, upper], ya_s.at[k, 3], ya_r.at[k, 3], left)

    for j in range(N_TP):
        xfull[:, j * SHARD : (j + 1) * SHARD] = land[j, 0]
    w_copies[0].wait()
    w_copies[1].wait()
    zg = lax.dot_general(xfull[...], w[0], NT, preferred_element_type=F32)
    zu = lax.dot_general(xfull[...], w[1], NT, preferred_element_type=F32)
    sig = jax.nn.sigmoid(zg)
    active = zg * sig
    y_send(2, active * zu)
    act_f[0] = active
    act_f[1] = zu * sig * (1.0 + zg * (1.0 - sig))

    forward(1, 1)
    y_forward(2)
    slices(1, 1)
    core_slice(1)
    for j in range(N_TP):
        gfull[:, j * SHARD : (j + 1) * SHARD] = land[j, 1]
    w_copies[2].wait()
    dh = lax.dot_general(gfull[...], w[2], NT, preferred_element_type=F32)
    y_send(1, dh * act_f[0])
    y_send(0, dh * act_f[1])

    def ig_multiply():
        def masked(k):
            return jnp.concatenate(
                [
                    ab[y, k, s * TOK : (s + 1) * TOK] * jnp.full((TOK, BLOCK), fill[s], F32).astype(BF16)
                    for s in range(SLOTS)
                ],
                axis=1,
            )

        gate_m, up_m = masked(0), masked(1)
        for p in range(N_TP // 2):
            cols = slice(p * 2 * SHARD, (p + 1) * 2 * SHARD)
            value = (
                jnp.dot(gate_m, w[0, :, cols], preferred_element_type=F32)
                + jnp.dot(up_m, w[1, :, cols], preferred_element_type=F32)
            ).astype(BF16)
            ig_send[2 * p] = value[:, :SHARD]
            ig_send[2 * p + 1] = value[:, SHARD:]

    def select(k, owner, i):
        spot = place[owner * 2 + i]
        total = None
        for yt in range(N_Y):
            for s in range(SLOTS):
                m = jnp.where(spot == at(zh, yt) * SLOTS + s, 1.0, 0.0)
                term = ab[yt, k, s * TOK : (s + 1) * TOK] * jnp.full((TOK, BLOCK), m, F32).astype(BF16)
                total = term if total is None else total + term
        return total

    az = {}

    def y_select(k):
        ya[k, 2].wait_recv()
        ya[k, 3].wait_recv()
        for i in range(2):
            az_send[k, i] = select(k, anti, i)
        az[k] = start(az_send.at[k], az_land.at[k], az_s.at[k], az_r.at[k], anti_dev)
        for i in range(2):
            own_sel[k, i] = select(k, tp, i)

    x_right, x_left = group_dev(x_at(1), c), group_dev(x_at(3), c)
    top, bottom = pl.ds(0, BLOCK), pl.ds(BLOCK, BLOCK)
    xa = {}

    def x_send(k, q, ref, dev):
        xa[k, q] = start(ref, ref, xa_s.at[k, q], xa_r.at[k, q], dev)

    def x_first(k):
        az[k].wait_recv()
        for i in range(2):
            ftb[me, k, i * BLOCK : (i + 1) * BLOCK, :] = (own_sel[k, i] + az_land[k, i]).T
        x_send(k, 0, ftb.at[me, k], x_right)
        x_send(k, 1, ftb.at[me, k], x_left)
        x_send(k, 4, ftb.at[me, k], core_dev)

    def x_forward(k):
        xa[k, 0].wait_recv()
        x_send(k, 2, ftb.at[c * 4 + x_at(3), k, top], x_right)
        x_send(k, 5, ftb.at[c * 4 + x_at(3), k], core_dev)
        xa[k, 1].wait_recv()
        x_send(k, 3, ftb.at[c * 4 + x_at(1), k, bottom], x_left)
        x_send(k, 6, ftb.at[c * 4 + x_at(1), k], core_dev)

    def x_last(k):
        xa[k, 2].wait_recv()
        xa[k, 3].wait_recv()
        x_send(k, 7, ftb.at[c * 4 + x_at(2), k], core_dev)

    zz = {}

    def z_first(k):
        for q in (4, 5, 6, 7):
            xa[k, q].wait_recv()
        a = 0 if k < 2 else 1
        total = None
        for g in range(GROUP):
            term = jnp.dot(ftb[g, k], xl[g, a], preferred_element_type=F32)
            total = term if total is None else total + term
        for zt in range(N_ZL):
            piece = total[zt * 64 : (zt + 1) * 64]
            part[k, zt] = piece
            z_send[k, zt] = piece.astype(BF16)
        for j in (2, 1, 3):
            zz[k, j] = start(
                z_send.at[k, lax.rem(zl + j, 4)], z_land.at[k, j - 1], z_s.at[k, j - 1], z_r.at[k, j - 1], z_dev(j)
            )

    rows = {}

    def rows_first(k):
        for j in (1, 2, 3):
            zz[k, j].wait_recv()
        value = (part[k, zl] + z_land[k, 0].astype(F32)) + (z_land[k, 1].astype(F32) + z_land[k, 2].astype(F32))
        tr[k] = (value * (1.0 / REPLICAS)).reshape(GROUP, 8, SHARD)
        for r in range(1, GROUP):
            q = lax.rem(seat + r, GROUP)
            rows[k, r] = start(
                tr.at[k, q], gl.at[k, me], tr_s.at[k, r - 1], tr_r.at[k, r - 1], group_dev(lax.div(q, 2), lax.rem(q, 2))
            )
        gl[k, me] = tr[k, seat]

    def rows_last(k):
        for r in range(1, GROUP):
            rows[k, r].wait_recv()
        for g in range(GROUP):
            grad_out[k, :, g * SHARD : (g + 1) * SHARD] = gl[k, g]

    ig = {}

    def ig_first():
        for half, zt in ((0, oh), (1, zh)):
            for j in (2, 1, 3):
                ig[half, j] = start(
                    ig_send.at[at(zt, lax.rem(y + j, 4))],
                    ig_land.at[j - 1, half],
                    ig_s.at[j - 1, half],
                    ig_r.at[j - 1, half],
                    y_dev(j),
                )

    def ig_sum(half, owner):
        for j in (1, 2, 3):
            ig[half, j].wait_recv()
        return (ig_send[owner].astype(F32) + ig_land[0, half].astype(F32)) + (
            ig_land[1, half].astype(F32) + ig_land[2, half].astype(F32)
        )

    def slices_wait():
        for r in range(1, GROUP):
            g = lax.rem(me + r, GROUP)
            for a in range(2):
                remote(xl.at[g, a], xl.at[g, a], xs_s.at[r - 1, a], xs_r.at[g, a], core_dev).wait_recv()

    y_select(2)
    ig_multiply()
    xl[me] = land[me]
    y_forward(1)
    y_forward(0)
    x_first(2)
    y_select(1)
    y_select(0)
    ig_first()
    x_forward(2)
    x_last(2)
    x_first(1)
    slices_wait()
    z_first(2)
    x_first(0)
    x_forward(1)
    ig_zsend[...] = ig_sum(0, anti).astype(BF16)
    iz = start(ig_zsend, ig_zland, iz_s, iz_r, anti_dev)
    x_last(1)
    x_forward(0)
    z_first(1)
    rows_first(2)
    x_last(0)
    z_first(0)
    ig_own[...] = ig_sum(1, tp)
    rows_first(1)
    rows_last(2)
    rows_first(0)
    rows_last(1)
    rows_last(0)
    iz.wait_recv()
    ig_out[...] = (ig_own[...] + ig_zland[...].astype(F32)).astype(BF16)

    for cp in sent:
        cp.wait_send()


def adam(ig, grad, master, mom_one, mom_two, ig_out, master_out, one_out, two_out):
    ig_out[...] = ig[...]
    one = beta_one * mom_one[...] + (1.0 - beta_one) * grad[...]
    two = beta_two * mom_two[...] + (1.0 - beta_two) * grad[...] * grad[...]
    update = one / bias_one / (jnp.sqrt(two / bias_two) + adam_eps) + decay_rate * master[...]
    master_out[...] = master[...] - learn_rate * update
    one_out[...] = one
    two_out[...] = two


def per_device(tokens, cotangent, working, degraded, block_map, master, moment_one, moment_two):
    vmem = pl.BlockSpec(memory_space=pltpu.VMEM)
    smem = pl.BlockSpec(memory_space=pltpu.SMEM)
    hbm = pl.BlockSpec(memory_space=pltpu.HBM)
    dma = pltpu.SemaphoreType.DMA
    rows = jax.ShapeDtypeStruct((3, 8, D), F32)
    shard = jax.ShapeDtypeStruct((TOK, SHARD), BF16)
    ig, grad = pl.pallas_call(
        kernel,
        name="swiglu_step",
        out_shape=(shard, rows),
        in_specs=[hbm, hbm, hbm, smem, smem],
        out_specs=(vmem, vmem),
        scratch_shapes=[
            pltpu.VMEM((3, SLOTS * BLOCK, D), BF16),
            pltpu.VMEM((N_TP, 2, TOK, SHARD), BF16),
            pltpu.VMEM((GROUP, 2, TOK, SHARD), BF16),
            pltpu.VMEM((TOK, D), BF16),
            pltpu.VMEM((TOK, D), BF16),
            pltpu.SMEM((BLOCKS,), jnp.int32),
            pltpu.SMEM((SLOTS,), F32),
            pltpu.VMEM((N_Y, 3, UNIT, BLOCK), BF16),
            pltpu.VMEM((3, 2, TOK, BLOCK), BF16),
            pltpu.VMEM((3, 2, TOK, BLOCK), BF16),
            pltpu.VMEM((3, 2, TOK, BLOCK), BF16),
            pltpu.VMEM((GROUP, 3, 2 * BLOCK, TOK), BF16),
            pltpu.VMEM((N_TP, TOK, SHARD), BF16),
            pltpu.VMEM((3, 2, TOK, SHARD), BF16),
            pltpu.VMEM((TOK, SHARD), BF16),
            pltpu.VMEM((TOK, SHARD), BF16),
            pltpu.VMEM((TOK, SHARD), F32),
            pltpu.VMEM((2, TOK, SLOTS * BLOCK), F32),
            pltpu.VMEM((3, N_ZL, 64, SHARD), F32),
            pltpu.VMEM((3, N_ZL, 64, SHARD), BF16),
            pltpu.VMEM((3, 3, 64, SHARD), BF16),
            pltpu.VMEM((3, GROUP, 8, SHARD), F32),
            pltpu.VMEM((3, GROUP, 8, SHARD), F32),
            dma((5,)),
            dma((2, 9)),
            dma((2, 9)),
            dma((7, 2)),
            dma((GROUP, 2)),
            dma((3, 4)),
            dma((3, 4)),
            dma((3,)),
            dma((3,)),
            dma((3, 8)),
            dma((3, 8)),
            dma((3, 2)),
            dma((3, 2)),
            dma,
            dma,
            dma((3, 3)),
            dma((3, 3)),
            dma((3, GROUP - 1)),
            dma((3, GROUP - 1)),
        ],
        compiler_params=pltpu.CompilerParams(
            collective_id=0, has_side_effects=True, vmem_limit_bytes=55 * 1024 * 1024
        ),
        cost_estimate=pl.CostEstimate(flops=3_700_000_000, bytes_accessed=12_000_000, transcendentals=73728),
    )(tokens, cotangent, working.reshape(working.shape[2:]), degraded, block_map)
    return pl.pallas_call(
        adam,
        name="adamw",
        out_shape=(shard, rows, rows, rows),
        in_specs=[vmem] * 5,
        out_specs=(vmem,) * 4,
        compiler_params=pltpu.CompilerParams(vmem_limit_bytes=8 * 1024 * 1024),
    )(ig, grad, master, moment_one, moment_two)


def solution(mesh):
    return jax.shard_map(
        per_device,
        mesh=mesh,
        in_specs=(
            P("dp", "tp"),
            P("dp", "tp"),
            P("dp", "tp", None, None, None),
            P("dp"),
            P("dp", None),
            P(None, ("tp", "dp"), None),
            P(None, ("tp", "dp"), None),
            P(None, ("tp", "dp"), None),
        ),
        out_specs=(
            P("dp", "tp"),
            P(None, ("tp", "dp"), None),
            P(None, ("tp", "dp"), None),
            P(None, ("tp", "dp"), None),
        ),
        check_vma=False,
    )
```

```python
import jax
import jax.numpy as jnp
from jax import lax
from jax.experimental import pallas as pl
from jax.experimental.pallas import tpu as pltpu
from jax.sharding import PartitionSpec as P

MESH = pl.DeviceIdType.MESH
F32, BF16 = jnp.float32, jnp.bfloat16

D = 3584
BLOCK = 128
BLOCKS = 16
SLOTS = 3
TOK = 192
N_Y, N_ZH, N_X, N_ZL = 4, 2, 4, 4
N_TP = N_Y * N_ZH
REPLICAS = N_X * N_ZL * 2
SHARD = D // N_TP
GROUP = 2 * N_X
UNIT = SLOTS * TOK
PACKED = TOK * SHARD // BLOCK
EARLY, LATE = (0, PACKED // 2), (PACKED // 2, PACKED // 2)
Z_ROWS = 64
Z_PACKED = Z_ROWS * SHARD // BLOCK

beta_one = 0.9
beta_two = 0.95
learn_rate = 0.05
decay_rate = 0.1
adam_eps = 1e-08
bias_one = 1.0 - 0.9**10
bias_two = 1.0 - 0.95**10

NT = (((1,), (1,)), ((), ()))


def pack(value):
    half = value.shape[0] // 2
    tiles = [value[:, t * BLOCK : (t + 1) * BLOCK] for t in range(3)]
    return jnp.concatenate(tiles + [jnp.concatenate([value[:half, 3 * BLOCK :], value[half:, 3 * BLOCK :]], axis=1)], axis=0)


def unpack(value):
    rows = value.shape[0] * BLOCK // SHARD
    tiles = [value[t * rows : (t + 1) * rows] for t in range(3)]
    last = value[3 * rows :]
    return jnp.concatenate(tiles + [jnp.concatenate([last[:, :64], last[:, 64:]], axis=0)], axis=1)


def kernel(
    tok, cot, work, flag, bmap,
    ig_out, grad_out,
    w, raw, land, xl, xfull, gfull,
    place, fill, ab, own_sel, az_send, az_land, ftb,
    ig_send, ig_land, ig_zsend, ig_zland, ig_own, act_f,
    part, z_send, z_land, tr, gl,
    w_sem, p1_s, p1_r, xs_s, xs_r,
    ya_s, ya_r, az_s, az_r, xa_s, xa_r,
    ig_s, ig_r, iz_s, iz_r,
    z_s, z_r, tr_s, tr_r,
):
    dp, tp = lax.axis_index("dp"), lax.axis_index("tp")
    zl, x, c = lax.div(dp, 8), lax.rem(lax.div(dp, 2), 4), lax.rem(dp, 2)
    zh, y = lax.div(tp, 4), lax.rem(tp, 4)
    oh = 1 - zh
    oc = 1 - c
    me = c * 4 + x
    seat = x * 2 + c

    def at(zh_, y_):
        return zh_ * 4 + y_

    def y_dev(j):
        return (dp, at(zh, lax.rem(y + j, 4)))

    def group_dev(x_, c_):
        return (zl * 8 + x_ * 2 + c_, tp)

    def z_dev(j):
        return (lax.rem(zl + j, 4) * 8 + x * 2 + c, tp)

    def x_at(j):
        return lax.rem(x + j, 4)

    anti = at(oh, y)
    anti_dev = (dp, anti)
    core_dev = group_dev(x, oc)

    def remote(src, dst, ssem, rsem, dev):
        return pltpu.make_async_remote_copy(
            src_ref=src, dst_ref=dst, send_sem=ssem, recv_sem=rsem, device_id=dev, device_id_type=MESH
        )

    sent = []

    def start(src, dst, ssem, rsem, dev):
        cp = remote(src, dst, ssem, rsem, dev)
        cp.start()
        sent.append(cp)
        return cp

    barrier = pltpu.get_barrier_semaphore()
    partners = [y_dev(1), y_dev(2), y_dev(3), anti_dev, core_dev]
    partners += [group_dev(x_at(j), t) for j in (1, 2, 3) for t in (c, oc)]
    partners += [z_dev(1), z_dev(2), z_dev(3)]
    for dev in partners:
        pl.semaphore_signal(barrier, inc=1, device_id=dev, device_id_type=MESH)

    own_copies = [pltpu.make_async_copy(ref, raw.at[a], w_sem.at[3 + a]) for a, ref in ((0, tok), (1, cot))]
    for cp in own_copies:
        cp.start()
    w_copies = [pltpu.make_async_copy(work.at[k], w.at[k], w_sem.at[k]) for k in range(3)]
    for cp in w_copies:
        cp.start()

    holders = [jnp.where(flag[0] > 0, bmap[0, b], b // 2) for b in range(BLOCKS)]
    filled = [jnp.float32(0.0)] * SLOTS
    for b in range(BLOCKS):
        rank = jnp.int32(0)
        for e in range(b):
            rank = rank + jnp.where(holders[e] == holders[b], 1, 0)
        spot = holders[b] * SLOTS + rank
        place[b] = spot
        for s in range(SLOTS):
            filled[s] = filled[s] + jnp.where(spot == tp * SLOTS + s, 1.0, 0.0)
    for s in range(SLOTS):
        fill[s] = filled[s]

    for a in range(2):
        own_copies[a].wait()
        land[tp, a] = pack(raw[a])
    pl.semaphore_wait(barrier, len(partners))

    right, left = y_dev(1), y_dev(3)
    yr, yl = lax.rem(y + 1, 4), lax.rem(y + 3, 4)
    p1 = {}

    def send(a, index, chunk, dev, rows=(0, PACKED)):
        ref = land.at[chunk, a, pl.ds(*rows)]
        p1[a, index] = start(ref, ref, p1_s.at[a, index], p1_r.at[a, index], dev)

    def neighbours(a, half):
        chunk = (tp, anti)[half]
        send(a, 1 + 4 * half, chunk, right)
        send(a, 2 + 4 * half, chunk, left)

    def forward(a, half):
        zt = (zh, oh)[half]
        p1[a, 1 + 4 * half].wait_recv()
        send(a, 3 + 4 * half, at(zt, yl), right, EARLY)
        p1[a, 2 + 4 * half].wait_recv()
        send(a, 4 + 4 * half, at(zt, yr), left, LATE)

    def slices(a, half):
        p1[a, 3 + 4 * half].wait_recv()
        p1[a, 4 + 4 * half].wait_recv()
        zt = (zh, oh)[half]
        for j in (2, 1, 3):
            start(
                land.at[at(zt, x_at(j)), a],
                xl.at[me, a],
                xs_s.at[half * 3 + j - 1, a],
                xs_r.at[me, a],
                group_dev(x_at(j), zt),
            )

    def core_slice(a):
        start(land.at[oc * 4 + x, a], xl.at[me, a], xs_s.at[6, a], xs_r.at[me, a], core_dev)

    send(0, 0, tp, anti_dev)
    neighbours(0, 0)
    send(1, 0, tp, anti_dev)
    forward(0, 0)
    neighbours(1, 0)
    p1[0, 0].wait_recv()
    neighbours(0, 1)
    forward(1, 0)
    slices(0, 0)
    forward(0, 1)
    p1[1, 0].wait_recv()
    neighbours(1, 1)
    slices(1, 0)
    slices(0, 1)
    core_slice(0)

    ya = {}

    def y_send(k, value):
        value = value.astype(BF16)
        for s in range(SLOTS):
            ab[y, k, s * TOK : (s + 1) * TOK] = value[:, s * BLOCK : (s + 1) * BLOCK]
        for q, dev in ((0, right), (1, left)):
            ya[k, q] = start(ab.at[y, k], ab.at[y, k], ya_s.at[k, q], ya_r.at[k, q], dev)

    lower, upper = pl.ds(0, UNIT // 2), pl.ds(UNIT // 2, UNIT // 2)

    def y_forward(k):
        ya[k, 0].wait_recv()
        ya[k, 2] = start(ab.at[yl, k, lower], ab.at[yl, k, lower], ya_s.at[k, 2], ya_r.at[k, 2], right)
        ya[k, 1].wait_recv()
        ya[k, 3] = start(ab.at[yr, k, upper], ab.at[yr, k, upper], ya_s.at[k, 3], ya_r.at[k, 3], left)

    for j in range(N_TP):
        xfull[:, j * SHARD : (j + 1) * SHARD] = unpack(land[j, 0])
    w_copies[0].wait()
    w_copies[1].wait()
    zg = lax.dot_general(xfull[...], w[0], NT, preferred_element_type=F32)
    zu = lax.dot_general(xfull[...], w[1], NT, preferred_element_type=F32)
    sig = jax.nn.sigmoid(zg)
    active = zg * sig
    y_send(2, active * zu)
    act_f[0] = active
    act_f[1] = zu * sig * (1.0 + zg * (1.0 - sig))

    forward(1, 1)
    y_forward(2)
    slices(1, 1)
    core_slice(1)
    for j in range(N_TP):
        gfull[:, j * SHARD : (j + 1) * SHARD] = unpack(land[j, 1])
    w_copies[2].wait()
    dh = lax.dot_general(gfull[...], w[2], NT, preferred_element_type=F32)
    y_send(1, dh * act_f[0])
    y_send(0, dh * act_f[1])

    def ig_multiply():
        def masked(k):
            return jnp.concatenate(
                [
                    ab[y, k, s * TOK : (s + 1) * TOK] * jnp.full((TOK, BLOCK), fill[s], F32).astype(BF16)
                    for s in range(SLOTS)
                ],
                axis=1,
            )

        gate_m, up_m = masked(0), masked(1)
        for p in range(N_TP // 2):
            cols = slice(p * 2 * SHARD, (p + 1) * 2 * SHARD)
            value = (
                jnp.dot(gate_m, w[0, :, cols], preferred_element_type=F32)
                + jnp.dot(up_m, w[1, :, cols], preferred_element_type=F32)
            ).astype(BF16)
            ig_send[2 * p] = pack(value[:, :SHARD])
            ig_send[2 * p + 1] = pack(value[:, SHARD:])

    def select(k, owner, i):
        spot = place[owner * 2 + i]
        total = None
        for yt in range(N_Y):
            for s in range(SLOTS):
                m = jnp.where(spot == at(zh, yt) * SLOTS + s, 1.0, 0.0)
                term = ab[yt, k, s * TOK : (s + 1) * TOK] * jnp.full((TOK, BLOCK), m, F32).astype(BF16)
                total = term if total is None else total + term
        return total

    az = {}

    def y_select(k):
        ya[k, 2].wait_recv()
        ya[k, 3].wait_recv()
        for i in range(2):
            az_send[k, i] = select(k, anti, i)
        az[k] = start(az_send.at[k], az_land.at[k], az_s.at[k], az_r.at[k], anti_dev)
        for i in range(2):
            own_sel[k, i] = select(k, tp, i)

    x_right, x_left = group_dev(x_at(1), c), group_dev(x_at(3), c)
    top, bottom = pl.ds(0, TOK), pl.ds(TOK, TOK)
    xa = {}

    def x_send(k, q, ref, dev):
        xa[k, q] = start(ref, ref, xa_s.at[k, q], xa_r.at[k, q], dev)

    def x_first(k):
        az[k].wait_recv()
        block = [(own_sel[k, i] + az_land[k, i]).T for i in range(2)]
        ftb[me, k, :BLOCK] = block[0][:, :BLOCK]
        ftb[me, k, BLOCK : 2 * BLOCK] = block[1][:, :BLOCK]
        ftb[me, k, 2 * BLOCK :] = jnp.concatenate([block[0][:, BLOCK:], block[1][:, BLOCK:]], axis=1)
        x_send(k, 0, ftb.at[me, k], x_right)
        x_send(k, 1, ftb.at[me, k], x_left)
        x_send(k, 4, ftb.at[me, k], core_dev)

    def x_forward(k):
        xa[k, 0].wait_recv()
        x_send(k, 2, ftb.at[c * 4 + x_at(3), k, top], x_right)
        x_send(k, 5, ftb.at[c * 4 + x_at(3), k], core_dev)
        xa[k, 1].wait_recv()
        x_send(k, 3, ftb.at[c * 4 + x_at(1), k, bottom], x_left)
        x_send(k, 6, ftb.at[c * 4 + x_at(1), k], core_dev)

    def x_last(k):
        xa[k, 2].wait_recv()
        xa[k, 3].wait_recv()
        x_send(k, 7, ftb.at[c * 4 + x_at(2), k], core_dev)

    zz = {}

    def z_first(k):
        for q in (4, 5, 6, 7):
            xa[k, q].wait_recv()
        a = 0 if k < 2 else 1
        total = None
        for g in range(GROUP):
            last = ftb[g, k, 2 * BLOCK :]
            lhs = jnp.concatenate(
                [
                    jnp.concatenate([ftb[g, k, :BLOCK], last[:, :64]], axis=1),
                    jnp.concatenate([ftb[g, k, BLOCK : 2 * BLOCK], last[:, 64:]], axis=1),
                ],
                axis=0,
            )
            term = jnp.dot(lhs, unpack(xl[g, a]), preferred_element_type=F32)
            total = term if total is None else total + term
        for zt in range(N_ZL):
            piece = total[zt * Z_ROWS : (zt + 1) * Z_ROWS]
            part[k, zt] = piece
            z_send[k, zt] = pack(piece.astype(BF16))
        for j in (2, 1, 3):
            zz[k, j] = start(
                z_send.at[k, lax.rem(zl + j, 4)], z_land.at[k, j - 1], z_s.at[k, j - 1], z_r.at[k, j - 1], z_dev(j)
            )

    rows = {}

    def rows_first(k):
        for j in (1, 2, 3):
            zz[k, j].wait_recv()
        others = z_land[k, 0].astype(F32) + z_land[k, 1].astype(F32) + z_land[k, 2].astype(F32)
        value = part[k, zl] + unpack(others)
        tr[k] = (value * (1.0 / REPLICAS)).reshape(GROUP, 8, SHARD)
        for r in range(1, GROUP):
            q = lax.rem(seat + r, GROUP)
            rows[k, r] = start(
                tr.at[k, q], gl.at[k, me], tr_s.at[k, r - 1], tr_r.at[k, r - 1], group_dev(lax.div(q, 2), lax.rem(q, 2))
            )
        gl[k, me] = tr[k, seat]

    def rows_last(k):
        for r in range(1, GROUP):
            rows[k, r].wait_recv()
        for g in range(GROUP):
            grad_out[k, :, g * SHARD : (g + 1) * SHARD] = gl[k, g]

    ig = {}

    def ig_first():
        for half, zt in ((0, oh), (1, zh)):
            for j in (2, 1, 3):
                ig[half, j] = start(
                    ig_send.at[at(zt, lax.rem(y + j, 4))],
                    ig_land.at[j - 1, half],
                    ig_s.at[j - 1, half],
                    ig_r.at[j - 1, half],
                    y_dev(j),
                )

    def ig_sum(half, owner):
        for j in (1, 2, 3):
            ig[half, j].wait_recv()
        return (ig_send[owner].astype(F32) + ig_land[0, half].astype(F32)) + (
            ig_land[1, half].astype(F32) + ig_land[2, half].astype(F32)
        )

    def slices_wait():
        for r in range(1, GROUP):
            g = lax.rem(me + r, GROUP)
            for a in range(2):
                remote(xl.at[g, a], xl.at[g, a], xs_s.at[r - 1, a], xs_r.at[g, a], core_dev).wait_recv()

    y_select(2)
    ig_multiply()
    xl[me] = land[me]
    y_forward(1)
    y_forward(0)
    x_first(2)
    y_select(1)
    y_select(0)
    ig_first()
    x_forward(2)
    x_last(2)
    x_first(1)
    slices_wait()
    z_first(2)
    x_first(0)
    x_forward(1)
    ig_zsend[...] = ig_sum(0, anti).astype(BF16)
    iz = start(ig_zsend, ig_zland, iz_s, iz_r, anti_dev)
    x_last(1)
    x_forward(0)
    z_first(1)
    rows_first(2)
    x_last(0)
    z_first(0)
    ig_own[...] = ig_sum(1, tp)
    rows_first(1)
    rows_last(2)
    rows_first(0)
    rows_last(1)
    rows_last(0)
    iz.wait_recv()
    ig_out[...] = unpack((ig_own[...] + ig_zland[...].astype(F32)).astype(BF16))

    for cp in sent:
        cp.wait_send()


def adam(ig, grad, master, mom_one, mom_two, ig_out, master_out, one_out, two_out):
    ig_out[...] = ig[...]
    one = beta_one * mom_one[...] + (1.0 - beta_one) * grad[...]
    two = beta_two * mom_two[...] + (1.0 - beta_two) * grad[...] * grad[...]
    update = one / bias_one / (jnp.sqrt(two / bias_two) + adam_eps) + decay_rate * master[...]
    master_out[...] = master[...] - learn_rate * update
    one_out[...] = one
    two_out[...] = two


def per_device(tokens, cotangent, working, degraded, block_map, master, moment_one, moment_two):
    vmem = pl.BlockSpec(memory_space=pltpu.VMEM)
    smem = pl.BlockSpec(memory_space=pltpu.SMEM)
    hbm = pl.BlockSpec(memory_space=pltpu.HBM)
    dma = pltpu.SemaphoreType.DMA
    rows = jax.ShapeDtypeStruct((3, 8, D), F32)
    shard = jax.ShapeDtypeStruct((TOK, SHARD), BF16)
    ig, grad = pl.pallas_call(
        kernel,
        name="swiglu_step",
        out_shape=(shard, rows),
        in_specs=[hbm, hbm, hbm, smem, smem],
        out_specs=(vmem, vmem),
        scratch_shapes=[
            pltpu.VMEM((3, SLOTS * BLOCK, D), BF16),
            pltpu.VMEM((2, TOK, SHARD), BF16),
            pltpu.VMEM((N_TP, 2, PACKED, BLOCK), BF16),
            pltpu.VMEM((GROUP, 2, PACKED, BLOCK), BF16),
            pltpu.VMEM((TOK, D), BF16),
            pltpu.VMEM((TOK, D), BF16),
            pltpu.SMEM((BLOCKS,), jnp.int32),
            pltpu.SMEM((SLOTS,), F32),
            pltpu.VMEM((N_Y, 3, UNIT, BLOCK), BF16),
            pltpu.VMEM((3, 2, TOK, BLOCK), BF16),
            pltpu.VMEM((3, 2, TOK, BLOCK), BF16),
            pltpu.VMEM((3, 2, TOK, BLOCK), BF16),
            pltpu.VMEM((GROUP, 3, 3 * BLOCK, BLOCK), BF16),
            pltpu.VMEM((N_TP, PACKED, BLOCK), BF16),
            pltpu.VMEM((3, 2, PACKED, BLOCK), BF16),
            pltpu.VMEM((PACKED, BLOCK), BF16),
            pltpu.VMEM((PACKED, BLOCK), BF16),
            pltpu.VMEM((PACKED, BLOCK), F32),
            pltpu.VMEM((2, TOK, SLOTS * BLOCK), F32),
            pltpu.VMEM((3, N_ZL, Z_ROWS, SHARD), F32),
            pltpu.VMEM((3, N_ZL, Z_PACKED, BLOCK), BF16),
            pltpu.VMEM((3, 3, Z_PACKED, BLOCK), BF16),
            pltpu.VMEM((3, GROUP, 8, SHARD), F32),
            pltpu.VMEM((3, GROUP, 8, SHARD), F32),
            dma((5,)),
            dma((2, 9)),
            dma((2, 9)),
            dma((7, 2)),
            dma((GROUP, 2)),
            dma((3, 4)),
            dma((3, 4)),
            dma((3,)),
            dma((3,)),
            dma((3, 8)),
            dma((3, 8)),
            dma((3, 2)),
            dma((3, 2)),
            dma,
            dma,
            dma((3, 3)),
            dma((3, 3)),
            dma((3, GROUP - 1)),
            dma((3, GROUP - 1)),
        ],
        compiler_params=pltpu.CompilerParams(
            collective_id=0, has_side_effects=True, vmem_limit_bytes=55 * 1024 * 1024
        ),
        cost_estimate=pl.CostEstimate(flops=3_700_000_000, bytes_accessed=12_000_000, transcendentals=73728),
    )(tokens, cotangent, working.reshape(working.shape[2:]), degraded, block_map)
    return pl.pallas_call(
        adam,
        name="adamw",
        out_shape=(shard, rows, rows, rows),
        in_specs=[vmem] * 5,
        out_specs=(vmem,) * 4,
        compiler_params=pltpu.CompilerParams(vmem_limit_bytes=55 * 1024 * 1024),
    )(ig, grad, master, moment_one, moment_two)


def solution(mesh):
    return jax.shard_map(
        per_device,
        mesh=mesh,
        in_specs=(
            P("dp", "tp"),
            P("dp", "tp"),
            P("dp", "tp", None, None, None),
            P("dp"),
            P("dp", None),
            P(None, ("tp", "dp"), None),
            P(None, ("tp", "dp"), None),
            P(None, ("tp", "dp"), None),
        ),
        out_specs=(
            P("dp", "tp"),
            P(None, ("tp", "dp"), None),
            P(None, ("tp", "dp"), None),
            P(None, ("tp", "dp"), None),
        ),
        check_vma=False,
    )
```

```python
import jax
import jax.numpy as jnp
from jax import lax
from jax.experimental import pallas as pl
from jax.experimental.pallas import tpu as pltpu
from jax.sharding import PartitionSpec as P

MESH = pl.DeviceIdType.MESH
F32, BF16 = jnp.float32, jnp.bfloat16

D = 3584
BLOCK = 128
BLOCKS = 16
SLOTS = 3
TOK = 192
N_Y, N_ZH, N_X, N_ZL = 4, 2, 4, 4
N_TP = N_Y * N_ZH
REPLICAS = N_X * N_ZL * 2
SHARD = D // N_TP
GROUP = 2 * N_X
UNIT = SLOTS * TOK
PACKED = TOK * SHARD // BLOCK
EARLY, LATE = (0, PACKED // 2), (PACKED // 2, PACKED // 2)
Z_ROWS = 64
Z_PACKED = Z_ROWS * SHARD // BLOCK

beta_one = 0.9
beta_two = 0.95
learn_rate = 0.05
decay_rate = 0.1
adam_eps = 1e-08
bias_one = 1.0 - 0.9**10
bias_two = 1.0 - 0.95**10

NT = (((1,), (1,)), ((), ()))


def pack(value):
    half = value.shape[0] // 2
    tiles = [value[:, t * BLOCK : (t + 1) * BLOCK] for t in range(3)]
    return jnp.concatenate(tiles + [jnp.concatenate([value[:half, 3 * BLOCK :], value[half:, 3 * BLOCK :]], axis=1)], axis=0)


def unpack(value):
    rows = value.shape[0] * BLOCK // SHARD
    tiles = [value[t * rows : (t + 1) * rows] for t in range(3)]
    last = value[3 * rows :]
    return jnp.concatenate(tiles + [jnp.concatenate([last[:, :64], last[:, 64:]], axis=0)], axis=1)


def kernel(
    tok, cot, work, flag, bmap,
    ig_out, grad_out,
    w, raw, land, xl, xfull, gfull,
    place, fill, ab, own_sel, az_send, az_land, ftb,
    ig_send, ig_land, ig_zsend, ig_zland, ig_own, act_f,
    part, z_send, z_land, tr, gl,
    w_sem, p1_s, p1_r, xs_s, xs_r,
    ya_s, ya_r, az_s, az_r, xa_s, xa_r,
    ig_s, ig_r, iz_s, iz_r,
    z_s, z_r, tr_s, tr_r,
):
    dp, tp = lax.axis_index("dp"), lax.axis_index("tp")
    zl, x, c = lax.div(dp, 8), lax.rem(lax.div(dp, 2), 4), lax.rem(dp, 2)
    zh, y = lax.div(tp, 4), lax.rem(tp, 4)
    oh = 1 - zh
    oc = 1 - c
    me = c * 4 + x
    seat = x * 2 + c

    def at(zh_, y_):
        return zh_ * 4 + y_

    def y_dev(j):
        return (dp, at(zh, lax.rem(y + j, 4)))

    def group_dev(x_, c_):
        return (zl * 8 + x_ * 2 + c_, tp)

    def z_dev(j):
        return (lax.rem(zl + j, 4) * 8 + x * 2 + c, tp)

    def x_at(j):
        return lax.rem(x + j, 4)

    anti = at(oh, y)
    anti_dev = (dp, anti)
    core_dev = group_dev(x, oc)

    def remote(src, dst, ssem, rsem, dev):
        return pltpu.make_async_remote_copy(
            src_ref=src, dst_ref=dst, send_sem=ssem, recv_sem=rsem, device_id=dev, device_id_type=MESH
        )

    sent = []

    def start(src, dst, ssem, rsem, dev):
        cp = remote(src, dst, ssem, rsem, dev)
        cp.start()
        sent.append(cp)
        return cp

    barrier = pltpu.get_barrier_semaphore()
    partners = [y_dev(1), y_dev(2), y_dev(3), anti_dev, core_dev]
    partners += [group_dev(x_at(j), t) for j in (1, 2, 3) for t in (c, oc)]
    partners += [z_dev(1), z_dev(2), z_dev(3)]
    for dev in partners:
        pl.semaphore_signal(barrier, inc=1, device_id=dev, device_id_type=MESH)

    own_copies = [pltpu.make_async_copy(ref, raw.at[a], w_sem.at[3 + a]) for a, ref in ((0, tok), (1, cot))]
    for cp in own_copies:
        cp.start()
    w_copies = [pltpu.make_async_copy(work.at[k], w.at[k], w_sem.at[k]) for k in range(3)]
    for cp in w_copies:
        cp.start()

    holders = [jnp.where(flag[0] > 0, bmap[0, b], b // 2) for b in range(BLOCKS)]
    filled = [jnp.float32(0.0)] * SLOTS
    for b in range(BLOCKS):
        rank = jnp.int32(0)
        for e in range(b):
            rank = rank + jnp.where(holders[e] == holders[b], 1, 0)
        spot = holders[b] * SLOTS + rank
        place[b] = spot
        for s in range(SLOTS):
            filled[s] = filled[s] + jnp.where(spot == tp * SLOTS + s, 1.0, 0.0)
    for s in range(SLOTS):
        fill[s] = filled[s]

    for a in range(2):
        own_copies[a].wait()
        land[tp, a] = pack(raw[a])
    pl.semaphore_wait(barrier, len(partners))

    right, left = y_dev(1), y_dev(3)
    yr, yl = lax.rem(y + 1, 4), lax.rem(y + 3, 4)
    p1 = {}

    def send(a, index, chunk, dev, rows=(0, PACKED)):
        ref = land.at[chunk, a, pl.ds(*rows)]
        p1[a, index] = start(ref, ref, p1_s.at[a, index], p1_r.at[a, index], dev)

    def neighbours(a, half):
        chunk = (tp, anti)[half]
        send(a, 1 + 4 * half, chunk, right)
        send(a, 2 + 4 * half, chunk, left)

    def forward(a, half):
        zt = (zh, oh)[half]
        p1[a, 1 + 4 * half].wait_recv()
        send(a, 3 + 4 * half, at(zt, yl), right, EARLY)
        p1[a, 2 + 4 * half].wait_recv()
        send(a, 4 + 4 * half, at(zt, yr), left, LATE)

    def slices(a, half):
        p1[a, 3 + 4 * half].wait_recv()
        p1[a, 4 + 4 * half].wait_recv()
        zt = (zh, oh)[half]
        for j in (2, 1, 3):
            start(
                land.at[at(zt, x_at(j)), a],
                xl.at[me, a],
                xs_s.at[half * 3 + j - 1, a],
                xs_r.at[me, a],
                group_dev(x_at(j), zt),
            )

    def core_slice(a):
        start(land.at[oc * 4 + x, a], xl.at[me, a], xs_s.at[6, a], xs_r.at[me, a], core_dev)

    send(0, 0, tp, anti_dev)
    neighbours(0, 0)
    send(1, 0, tp, anti_dev)
    forward(0, 0)
    neighbours(1, 0)
    p1[0, 0].wait_recv()
    neighbours(0, 1)
    forward(1, 0)
    slices(0, 0)
    forward(0, 1)
    p1[1, 0].wait_recv()
    neighbours(1, 1)
    slices(1, 0)
    slices(0, 1)
    core_slice(0)

    ya = {}

    def y_send(k, value):
        value = value.astype(BF16)
        for s in range(SLOTS):
            ab[y, k, s * TOK : (s + 1) * TOK] = value[:, s * BLOCK : (s + 1) * BLOCK]
        for q, dev in ((0, right), (1, left)):
            ya[k, q] = start(ab.at[y, k], ab.at[y, k], ya_s.at[k, q], ya_r.at[k, q], dev)

    lower, upper = pl.ds(0, UNIT // 2), pl.ds(UNIT // 2, UNIT // 2)

    def y_forward(k):
        ya[k, 0].wait_recv()
        ya[k, 2] = start(ab.at[yl, k, lower], ab.at[yl, k, lower], ya_s.at[k, 2], ya_r.at[k, 2], right)
        ya[k, 1].wait_recv()
        ya[k, 3] = start(ab.at[yr, k, upper], ab.at[yr, k, upper], ya_s.at[k, 3], ya_r.at[k, 3], left)

    for j in range(N_TP):
        xfull[:, j * SHARD : (j + 1) * SHARD] = unpack(land[j, 0])
    w_copies[0].wait()
    w_copies[1].wait()
    zg = lax.dot_general(xfull[...], w[0], NT, preferred_element_type=F32)
    zu = lax.dot_general(xfull[...], w[1], NT, preferred_element_type=F32)
    sig = jax.nn.sigmoid(zg)
    active = zg * sig
    y_send(2, active * zu)
    act_f[0] = active
    act_f[1] = zu * sig * (1.0 + zg * (1.0 - sig))

    forward(1, 1)
    y_forward(2)
    slices(1, 1)
    core_slice(1)
    for j in range(N_TP):
        gfull[:, j * SHARD : (j + 1) * SHARD] = unpack(land[j, 1])
    w_copies[2].wait()
    dh = lax.dot_general(gfull[...], w[2], NT, preferred_element_type=F32)
    y_send(1, dh * act_f[0])
    y_send(0, dh * act_f[1])

    def ig_multiply():
        def masked(k):
            return jnp.concatenate(
                [
                    ab[y, k, s * TOK : (s + 1) * TOK] * jnp.full((TOK, BLOCK), fill[s], F32).astype(BF16)
                    for s in range(SLOTS)
                ],
                axis=1,
            )

        gate_m, up_m = masked(0), masked(1)
        for p in range(N_TP // 2):
            cols = slice(p * 2 * SHARD, (p + 1) * 2 * SHARD)
            value = (
                jnp.dot(gate_m, w[0, :, cols], preferred_element_type=F32)
                + jnp.dot(up_m, w[1, :, cols], preferred_element_type=F32)
            ).astype(BF16)
            ig_send[2 * p] = pack(value[:, :SHARD])
            ig_send[2 * p + 1] = pack(value[:, SHARD:])

    def select(k, owner, i):
        spot = place[owner * 2 + i]
        total = None
        for yt in range(N_Y):
            for s in range(SLOTS):
                m = jnp.where(spot == at(zh, yt) * SLOTS + s, 1.0, 0.0)
                term = ab[yt, k, s * TOK : (s + 1) * TOK] * jnp.full((TOK, BLOCK), m, F32).astype(BF16)
                total = term if total is None else total + term
        return total

    az = {}

    def y_select(k):
        ya[k, 2].wait_recv()
        ya[k, 3].wait_recv()
        for i in range(2):
            az_send[k, i] = select(k, anti, i)
        az[k] = start(az_send.at[k], az_land.at[k], az_s.at[k], az_r.at[k], anti_dev)
        for i in range(2):
            own_sel[k, i] = select(k, tp, i)

    x_right, x_left = group_dev(x_at(1), c), group_dev(x_at(3), c)
    xa = {}

    def x_send(k, q, ref, dev):
        xa[k, q] = start(ref, ref, xa_s.at[k, q], xa_r.at[k, q], dev)

    def x_first(k):
        az[k].wait_recv()
        block = [(own_sel[k, i] + az_land[k, i]).T for i in range(2)]
        ftb[me, k, :BLOCK] = block[0][:, :BLOCK]
        ftb[me, k, BLOCK : 2 * BLOCK] = block[1][:, :BLOCK]
        ftb[me, k, 2 * BLOCK :] = jnp.concatenate([block[0][:, BLOCK:], block[1][:, BLOCK:]], axis=1)
        x_send(k, 0, ftb.at[me, k], x_right)
        x_send(k, 1, ftb.at[me, k], x_left)
        x_send(k, 2, ftb.at[me, k], group_dev(x_at(2), c))
        x_send(k, 4, ftb.at[me, k], core_dev)

    def x_forward(k):
        xa[k, 0].wait_recv()
        x_send(k, 5, ftb.at[c * 4 + x_at(3), k], core_dev)
        xa[k, 1].wait_recv()
        x_send(k, 6, ftb.at[c * 4 + x_at(1), k], core_dev)

    def x_last(k):
        xa[k, 2].wait_recv()
        x_send(k, 7, ftb.at[c * 4 + x_at(2), k], core_dev)

    zz = {}

    def z_first(k):
        for q in (4, 5, 6, 7):
            xa[k, q].wait_recv()
        a = 0 if k < 2 else 1
        total = None
        for g in range(GROUP):
            last = ftb[g, k, 2 * BLOCK :]
            lhs = jnp.concatenate(
                [
                    jnp.concatenate([ftb[g, k, :BLOCK], last[:, :64]], axis=1),
                    jnp.concatenate([ftb[g, k, BLOCK : 2 * BLOCK], last[:, 64:]], axis=1),
                ],
                axis=0,
            )
            term = jnp.dot(lhs, unpack(xl[g, a]), preferred_element_type=F32)
            total = term if total is None else total + term
        for zt in range(N_ZL):
            piece = total[zt * Z_ROWS : (zt + 1) * Z_ROWS]
            part[k, zt] = piece
            z_send[k, zt] = pack(piece.astype(BF16))
        for j in (2, 1, 3):
            zz[k, j] = start(
                z_send.at[k, lax.rem(zl + j, 4)], z_land.at[k, j - 1], z_s.at[k, j - 1], z_r.at[k, j - 1], z_dev(j)
            )

    rows = {}

    def rows_first(k):
        for j in (1, 2, 3):
            zz[k, j].wait_recv()
        others = z_land[k, 0].astype(F32) + z_land[k, 1].astype(F32) + z_land[k, 2].astype(F32)
        value = part[k, zl] + unpack(others)
        tr[k] = (value * (1.0 / REPLICAS)).reshape(GROUP, 8, SHARD)
        for r in range(1, GROUP):
            q = lax.rem(seat + r, GROUP)
            rows[k, r] = start(
                tr.at[k, q], gl.at[k, me], tr_s.at[k, r - 1], tr_r.at[k, r - 1], group_dev(lax.div(q, 2), lax.rem(q, 2))
            )
        gl[k, me] = tr[k, seat]

    def rows_last(k):
        for r in range(1, GROUP):
            rows[k, r].wait_recv()
        for g in range(GROUP):
            grad_out[k, :, g * SHARD : (g + 1) * SHARD] = gl[k, g]

    ig = {}

    def ig_first():
        for half, zt in ((0, oh), (1, zh)):
            for j in (2, 1, 3):
                ig[half, j] = start(
                    ig_send.at[at(zt, lax.rem(y + j, 4))],
                    ig_land.at[j - 1, half],
                    ig_s.at[j - 1, half],
                    ig_r.at[j - 1, half],
                    y_dev(j),
                )

    def ig_sum(half, owner):
        for j in (1, 2, 3):
            ig[half, j].wait_recv()
        return (ig_send[owner].astype(F32) + ig_land[0, half].astype(F32)) + (
            ig_land[1, half].astype(F32) + ig_land[2, half].astype(F32)
        )

    def slices_wait():
        for r in range(1, GROUP):
            g = lax.rem(me + r, GROUP)
            for a in range(2):
                remote(xl.at[g, a], xl.at[g, a], xs_s.at[r - 1, a], xs_r.at[g, a], core_dev).wait_recv()

    y_select(2)
    y_forward(1)
    ig_multiply()
    xl[me] = land[me]
    y_forward(0)
    x_first(2)
    y_select(1)
    y_select(0)
    x_forward(2)
    x_first(1)
    x_last(2)
    ig_first()
    x_first(0)
    slices_wait()
    z_first(2)
    x_forward(1)
    x_last(1)
    z_first(1)
    x_forward(0)
    rows_first(2)
    x_last(0)
    z_first(0)
    ig_zsend[...] = ig_sum(0, anti).astype(BF16)
    iz = start(ig_zsend, ig_zland, iz_s, iz_r, anti_dev)
    rows_first(1)
    ig_own[...] = ig_sum(1, tp)
    rows_last(2)
    rows_first(0)
    rows_last(1)
    rows_last(0)
    iz.wait_recv()
    ig_out[...] = unpack((ig_own[...] + ig_zland[...].astype(F32)).astype(BF16))

    for cp in sent:
        cp.wait_send()


def adam(ig, grad, master, mom_one, mom_two, ig_out, master_out, one_out, two_out):
    ig_out[...] = ig[...]
    one = beta_one * mom_one[...] + (1.0 - beta_one) * grad[...]
    two = beta_two * mom_two[...] + (1.0 - beta_two) * grad[...] * grad[...]
    update = one / bias_one / (jnp.sqrt(two / bias_two) + adam_eps) + decay_rate * master[...]
    master_out[...] = master[...] - learn_rate * update
    one_out[...] = one
    two_out[...] = two


def per_device(tokens, cotangent, working, degraded, block_map, master, moment_one, moment_two):
    vmem = pl.BlockSpec(memory_space=pltpu.VMEM)
    smem = pl.BlockSpec(memory_space=pltpu.SMEM)
    hbm = pl.BlockSpec(memory_space=pltpu.HBM)
    dma = pltpu.SemaphoreType.DMA
    rows = jax.ShapeDtypeStruct((3, 8, D), F32)
    shard = jax.ShapeDtypeStruct((TOK, SHARD), BF16)
    ig, grad = pl.pallas_call(
        kernel,
        name="swiglu_step",
        out_shape=(shard, rows),
        in_specs=[hbm, hbm, hbm, smem, smem],
        out_specs=(vmem, vmem),
        scratch_shapes=[
            pltpu.VMEM((3, SLOTS * BLOCK, D), BF16),
            pltpu.VMEM((2, TOK, SHARD), BF16),
            pltpu.VMEM((N_TP, 2, PACKED, BLOCK), BF16),
            pltpu.VMEM((GROUP, 2, PACKED, BLOCK), BF16),
            pltpu.VMEM((TOK, D), BF16),
            pltpu.VMEM((TOK, D), BF16),
            pltpu.SMEM((BLOCKS,), jnp.int32),
            pltpu.SMEM((SLOTS,), F32),
            pltpu.VMEM((N_Y, 3, UNIT, BLOCK), BF16),
            pltpu.VMEM((3, 2, TOK, BLOCK), BF16),
            pltpu.VMEM((3, 2, TOK, BLOCK), BF16),
            pltpu.VMEM((3, 2, TOK, BLOCK), BF16),
            pltpu.VMEM((GROUP, 3, 3 * BLOCK, BLOCK), BF16),
            pltpu.VMEM((N_TP, PACKED, BLOCK), BF16),
            pltpu.VMEM((3, 2, PACKED, BLOCK), BF16),
            pltpu.VMEM((PACKED, BLOCK), BF16),
            pltpu.VMEM((PACKED, BLOCK), BF16),
            pltpu.VMEM((PACKED, BLOCK), F32),
            pltpu.VMEM((2, TOK, SLOTS * BLOCK), F32),
            pltpu.VMEM((3, N_ZL, Z_ROWS, SHARD), F32),
            pltpu.VMEM((3, N_ZL, Z_PACKED, BLOCK), BF16),
            pltpu.VMEM((3, 3, Z_PACKED, BLOCK), BF16),
            pltpu.VMEM((3, GROUP, 8, SHARD), F32),
            pltpu.VMEM((3, GROUP, 8, SHARD), F32),
            dma((5,)),
            dma((2, 9)),
            dma((2, 9)),
            dma((7, 2)),
            dma((GROUP, 2)),
            dma((3, 4)),
            dma((3, 4)),
            dma((3,)),
            dma((3,)),
            dma((3, 8)),
            dma((3, 8)),
            dma((3, 2)),
            dma((3, 2)),
            dma,
            dma,
            dma((3, 3)),
            dma((3, 3)),
            dma((3, GROUP - 1)),
            dma((3, GROUP - 1)),
        ],
        compiler_params=pltpu.CompilerParams(
            collective_id=0, has_side_effects=True, vmem_limit_bytes=55 * 1024 * 1024
        ),
        cost_estimate=pl.CostEstimate(flops=3_700_000_000, bytes_accessed=12_000_000, transcendentals=73728),
    )(tokens, cotangent, working.reshape(working.shape[2:]), degraded, block_map)
    return pl.pallas_call(
        adam,
        name="adamw",
        out_shape=(shard, rows, rows, rows),
        in_specs=[vmem] * 5,
        out_specs=(vmem,) * 4,
        compiler_params=pltpu.CompilerParams(vmem_limit_bytes=55 * 1024 * 1024),
    )(ig, grad, master, moment_one, moment_two)


def solution(mesh):
    return jax.shard_map(
        per_device,
        mesh=mesh,
        in_specs=(
            P("dp", "tp"),
            P("dp", "tp"),
            P("dp", "tp", None, None, None),
            P("dp"),
            P("dp", None),
            P(None, ("tp", "dp"), None),
            P(None, ("tp", "dp"), None),
            P(None, ("tp", "dp"), None),
        ),
        out_specs=(
            P("dp", "tp"),
            P(None, ("tp", "dp"), None),
            P(None, ("tp", "dp"), None),
            P(None, ("tp", "dp"), None),
        ),
        check_vma=False,
    )
```

```python
import jax
import jax.numpy as jnp
from jax import lax
from jax.experimental import pallas as pl
from jax.experimental.pallas import tpu as pltpu
from jax.sharding import PartitionSpec as P

MESH = pl.DeviceIdType.MESH
F32, BF16 = jnp.float32, jnp.bfloat16

D = 3584
BLOCK = 128
BLOCKS = 16
SLOTS = 3
TOK = 192
N_Y, N_ZH, N_X, N_ZL = 4, 2, 4, 4
N_TP = N_Y * N_ZH
REPLICAS = N_X * N_ZL * 2
SHARD = D // N_TP
GROUP = 2 * N_X
UNIT = SLOTS * TOK
PACKED = TOK * SHARD // BLOCK
EARLY, LATE = (0, PACKED // 2), (PACKED // 2, PACKED // 2)
Z_ROWS = 64
Z_PACKED = Z_ROWS * SHARD // BLOCK

beta_one = 0.9
beta_two = 0.95
learn_rate = 0.05
decay_rate = 0.1
adam_eps = 1e-08
bias_one = 1.0 - 0.9**10
bias_two = 1.0 - 0.95**10

NT = (((1,), (1,)), ((), ()))


def pack(value):
    half = value.shape[0] // 2
    tiles = [value[:, t * BLOCK : (t + 1) * BLOCK] for t in range(3)]
    return jnp.concatenate(tiles + [jnp.concatenate([value[:half, 3 * BLOCK :], value[half:, 3 * BLOCK :]], axis=1)], axis=0)


def unpack(value):
    rows = value.shape[0] * BLOCK // SHARD
    tiles = [value[t * rows : (t + 1) * rows] for t in range(3)]
    last = value[3 * rows :]
    return jnp.concatenate(tiles + [jnp.concatenate([last[:, :64], last[:, 64:]], axis=0)], axis=1)


def kernel(
    tok, cot, work, flag, bmap,
    ig_out, grad_out,
    w, raw, land, xl, xfull, gfull,
    place, fill, ab, own_sel, az_send, az_land, ftb,
    ig_send, ig_land, ig_zsend, ig_zland, ig_own, act_f,
    part, z_send, z_land, tr, gl,
    w_sem, p1_s, p1_r, xs_s, xs_r,
    ya_s, ya_r, az_s, az_r, xa_s, xa_r,
    ig_s, ig_r, iz_s, iz_r,
    z_s, z_r, tr_s, tr_r,
):
    dp, tp = lax.axis_index("dp"), lax.axis_index("tp")
    zl, x, c = lax.div(dp, 8), lax.rem(lax.div(dp, 2), 4), lax.rem(dp, 2)
    zh, y = lax.div(tp, 4), lax.rem(tp, 4)
    oh = 1 - zh
    oc = 1 - c
    me = c * 4 + x
    seat = x * 2 + c

    def at(zh_, y_):
        return zh_ * 4 + y_

    def y_dev(j):
        return (dp, at(zh, lax.rem(y + j, 4)))

    def group_dev(x_, c_):
        return (zl * 8 + x_ * 2 + c_, tp)

    def z_dev(j):
        return (lax.rem(zl + j, 4) * 8 + x * 2 + c, tp)

    def x_at(j):
        return lax.rem(x + j, 4)

    anti = at(oh, y)
    anti_dev = (dp, anti)
    core_dev = group_dev(x, oc)

    def remote(src, dst, ssem, rsem, dev):
        return pltpu.make_async_remote_copy(
            src_ref=src, dst_ref=dst, send_sem=ssem, recv_sem=rsem, device_id=dev, device_id_type=MESH
        )

    sent = []

    def start(src, dst, ssem, rsem, dev):
        cp = remote(src, dst, ssem, rsem, dev)
        cp.start()
        sent.append(cp)
        return cp

    barrier = pltpu.get_barrier_semaphore()
    partners = [y_dev(1), y_dev(2), y_dev(3), anti_dev, core_dev]
    partners += [group_dev(x_at(j), t) for j in (1, 2, 3) for t in (c, oc)]
    partners += [z_dev(1), z_dev(2), z_dev(3)]
    for dev in partners:
        pl.semaphore_signal(barrier, inc=1, device_id=dev, device_id_type=MESH)

    own_copies = [pltpu.make_async_copy(ref, raw.at[a], w_sem.at[3 + a]) for a, ref in ((0, tok), (1, cot))]
    for cp in own_copies:
        cp.start()
    w_copies = [pltpu.make_async_copy(work.at[k], w.at[k], w_sem.at[k]) for k in range(3)]
    for cp in w_copies:
        cp.start()

    holders = [jnp.where(flag[0] > 0, bmap[0, b], b // 2) for b in range(BLOCKS)]
    filled = [jnp.float32(0.0)] * SLOTS
    for b in range(BLOCKS):
        rank = jnp.int32(0)
        for e in range(b):
            rank = rank + jnp.where(holders[e] == holders[b], 1, 0)
        spot = holders[b] * SLOTS + rank
        place[b] = spot
        for s in range(SLOTS):
            filled[s] = filled[s] + jnp.where(spot == tp * SLOTS + s, 1.0, 0.0)
    for s in range(SLOTS):
        fill[s] = filled[s]

    for a in range(2):
        own_copies[a].wait()
        land[tp, a] = pack(raw[a])
    pl.semaphore_wait(barrier, len(partners))

    right, left = y_dev(1), y_dev(3)
    yr, yl = lax.rem(y + 1, 4), lax.rem(y + 3, 4)
    p1 = {}

    def send(a, index, chunk, dev, rows=(0, PACKED)):
        ref = land.at[chunk, a, pl.ds(*rows)]
        p1[a, index] = start(ref, ref, p1_s.at[a, index], p1_r.at[a, index], dev)

    def neighbours(a, half):
        chunk = (tp, anti)[half]
        send(a, 1 + 4 * half, chunk, right)
        send(a, 2 + 4 * half, chunk, left)

    def forward(a, half):
        zt = (zh, oh)[half]
        p1[a, 1 + 4 * half].wait_recv()
        send(a, 3 + 4 * half, at(zt, yl), right, EARLY)
        p1[a, 2 + 4 * half].wait_recv()
        send(a, 4 + 4 * half, at(zt, yr), left, LATE)

    def slices(a, half):
        p1[a, 3 + 4 * half].wait_recv()
        p1[a, 4 + 4 * half].wait_recv()
        zt = (zh, oh)[half]
        for j in (2, 1, 3):
            start(
                land.at[at(zt, x_at(j)), a],
                xl.at[me, a],
                xs_s.at[half * 3 + j - 1, a],
                xs_r.at[me, a],
                group_dev(x_at(j), zt),
            )

    def core_slice(a):
        start(land.at[oc * 4 + x, a], xl.at[me, a], xs_s.at[6, a], xs_r.at[me, a], core_dev)

    send(0, 0, tp, anti_dev)
    neighbours(0, 0)
    send(1, 0, tp, anti_dev)
    forward(0, 0)
    neighbours(1, 0)
    p1[0, 0].wait_recv()
    neighbours(0, 1)
    forward(1, 0)
    slices(0, 0)
    forward(0, 1)
    p1[1, 0].wait_recv()
    neighbours(1, 1)
    slices(1, 0)
    slices(0, 1)
    core_slice(0)

    ya = {}

    def y_send(k, value):
        value = value.astype(BF16)
        for s in range(SLOTS):
            ab[y, k, s * TOK : (s + 1) * TOK] = value[:, s * BLOCK : (s + 1) * BLOCK]
        for q, dev in ((0, right), (1, left)):
            ya[k, q] = start(ab.at[y, k], ab.at[y, k], ya_s.at[k, q], ya_r.at[k, q], dev)

    lower, upper = pl.ds(0, UNIT // 2), pl.ds(UNIT // 2, UNIT // 2)

    def y_forward(k):
        ya[k, 0].wait_recv()
        ya[k, 2] = start(ab.at[yl, k, lower], ab.at[yl, k, lower], ya_s.at[k, 2], ya_r.at[k, 2], right)
        ya[k, 1].wait_recv()
        ya[k, 3] = start(ab.at[yr, k, upper], ab.at[yr, k, upper], ya_s.at[k, 3], ya_r.at[k, 3], left)

    for j in range(N_TP):
        xfull[:, j * SHARD : (j + 1) * SHARD] = unpack(land[j, 0])
    w_copies[0].wait()
    w_copies[1].wait()
    zg = lax.dot_general(xfull[...], w[0], NT, preferred_element_type=F32)
    zu = lax.dot_general(xfull[...], w[1], NT, preferred_element_type=F32)
    sig = jax.nn.sigmoid(zg)
    active = zg * sig
    y_send(2, active * zu)
    act_f[0] = active
    act_f[1] = zu * sig * (1.0 + zg * (1.0 - sig))

    forward(1, 1)
    y_forward(2)
    slices(1, 1)
    core_slice(1)
    for j in range(N_TP):
        gfull[:, j * SHARD : (j + 1) * SHARD] = unpack(land[j, 1])
    w_copies[2].wait()
    dh = lax.dot_general(gfull[...], w[2], NT, preferred_element_type=F32)
    y_send(1, dh * act_f[0])
    y_send(0, dh * act_f[1])

    def ig_multiply():
        def masked(k):
            return jnp.concatenate(
                [
                    ab[y, k, s * TOK : (s + 1) * TOK] * jnp.full((TOK, BLOCK), fill[s], F32).astype(BF16)
                    for s in range(SLOTS)
                ],
                axis=1,
            )

        gate_m, up_m = masked(0), masked(1)
        for p in range(N_TP // 2):
            cols = slice(p * 2 * SHARD, (p + 1) * 2 * SHARD)
            value = (
                jnp.dot(gate_m, w[0, :, cols], preferred_element_type=F32)
                + jnp.dot(up_m, w[1, :, cols], preferred_element_type=F32)
            ).astype(BF16)
            ig_send[2 * p] = pack(value[:, :SHARD])
            ig_send[2 * p + 1] = pack(value[:, SHARD:])

    def select(k, owner, i):
        spot = place[owner * 2 + i]
        total = None
        for yt in range(N_Y):
            for s in range(SLOTS):
                m = jnp.where(spot == at(zh, yt) * SLOTS + s, 1.0, 0.0)
                term = ab[yt, k, s * TOK : (s + 1) * TOK] * jnp.full((TOK, BLOCK), m, F32).astype(BF16)
                total = term if total is None else total + term
        return total

    az = {}

    def y_select(k):
        ya[k, 2].wait_recv()
        ya[k, 3].wait_recv()
        for i in range(2):
            az_send[k, i] = select(k, anti, i)
        az[k] = start(az_send.at[k], az_land.at[k], az_s.at[k], az_r.at[k], anti_dev)
        for i in range(2):
            own_sel[k, i] = select(k, tp, i)

    x_right, x_left = group_dev(x_at(1), c), group_dev(x_at(3), c)
    xa = {}

    def x_send(k, q, ref, dev):
        xa[k, q] = start(ref, ref, xa_s.at[k, q], xa_r.at[k, q], dev)

    def x_first(k):
        az[k].wait_recv()
        block = [(own_sel[k, i] + az_land[k, i]).T for i in range(2)]
        ftb[me, k, :BLOCK] = block[0][:, :BLOCK]
        ftb[me, k, BLOCK : 2 * BLOCK] = block[1][:, :BLOCK]
        ftb[me, k, 2 * BLOCK :] = jnp.concatenate([block[0][:, BLOCK:], block[1][:, BLOCK:]], axis=1)
        x_send(k, 0, ftb.at[me, k], x_right)
        x_send(k, 1, ftb.at[me, k], x_left)
        x_send(k, 2, ftb.at[me, k], group_dev(x_at(2), c))
        x_send(k, 4, ftb.at[me, k], core_dev)

    def x_forward(k):
        xa[k, 0].wait_recv()
        x_send(k, 5, ftb.at[c * 4 + x_at(3), k], core_dev)
        xa[k, 1].wait_recv()
        x_send(k, 6, ftb.at[c * 4 + x_at(1), k], core_dev)

    def x_last(k):
        xa[k, 2].wait_recv()
        x_send(k, 7, ftb.at[c * 4 + x_at(2), k], core_dev)

    zz = {}

    def z_first(k):
        for q in (4, 5, 6, 7):
            xa[k, q].wait_recv()
        a = 0 if k < 2 else 1
        total = None
        for g in range(GROUP):
            last = ftb[g, k, 2 * BLOCK :]
            lhs = jnp.concatenate(
                [
                    jnp.concatenate([ftb[g, k, :BLOCK], last[:, :64]], axis=1),
                    jnp.concatenate([ftb[g, k, BLOCK : 2 * BLOCK], last[:, 64:]], axis=1),
                ],
                axis=0,
            )
            term = jnp.dot(lhs, unpack(xl[g, a]), preferred_element_type=F32)
            total = term if total is None else total + term
        for zt in range(N_ZL):
            piece = total[zt * Z_ROWS : (zt + 1) * Z_ROWS]
            part[k, zt] = piece
            z_send[k, zt] = pack(piece.astype(BF16))
        for j in (2, 1, 3):
            zz[k, j] = start(
                z_send.at[k, lax.rem(zl + j, 4)], z_land.at[k, j - 1], z_s.at[k, j - 1], z_r.at[k, j - 1], z_dev(j)
            )

    rows = {}

    def rows_first(k):
        for j in (1, 2, 3):
            zz[k, j].wait_recv()
        others = z_land[k, 0].astype(F32) + z_land[k, 1].astype(F32) + z_land[k, 2].astype(F32)
        value = part[k, zl] + unpack(others)
        tr[k] = (value * (1.0 / REPLICAS)).reshape(GROUP, 8, SHARD)
        for r in range(1, GROUP):
            q = lax.rem(seat + r, GROUP)
            rows[k, r] = start(
                tr.at[k, q], gl.at[k, me], tr_s.at[k, r - 1], tr_r.at[k, r - 1], group_dev(lax.div(q, 2), lax.rem(q, 2))
            )
        gl[k, me] = tr[k, seat]

    def rows_last(k):
        for r in range(1, GROUP):
            rows[k, r].wait_recv()
        for g in range(GROUP):
            grad_out[k, :, g * SHARD : (g + 1) * SHARD] = gl[k, g]

    ig = {}

    def ig_first():
        for half, zt in ((0, oh), (1, zh)):
            for j in (2, 1, 3):
                ig[half, j] = start(
                    ig_send.at[at(zt, lax.rem(y + j, 4))],
                    ig_land.at[j - 1, half],
                    ig_s.at[j - 1, half],
                    ig_r.at[j - 1, half],
                    y_dev(j),
                )

    def ig_sum(half, owner):
        for j in (1, 2, 3):
            ig[half, j].wait_recv()
        return (ig_send[owner].astype(F32) + ig_land[0, half].astype(F32)) + (
            ig_land[1, half].astype(F32) + ig_land[2, half].astype(F32)
        )

    def slices_wait():
        for r in range(1, GROUP):
            g = lax.rem(me + r, GROUP)
            for a in range(2):
                remote(xl.at[g, a], xl.at[g, a], xs_s.at[r - 1, a], xs_r.at[g, a], core_dev).wait_recv()

    y_select(2)
    y_forward(1)
    ig_multiply()
    xl[me] = land[me]
    y_forward(0)
    x_first(2)
    y_select(1)
    y_select(0)
    x_forward(2)
    x_first(1)
    x_last(2)
    ig_first()
    x_first(0)
    slices_wait()
    z_first(2)
    x_forward(1)
    x_last(1)
    z_first(1)
    x_forward(0)
    rows_first(2)
    x_last(0)
    z_first(0)
    ig_zsend[...] = ig_sum(0, anti).astype(BF16)
    iz = start(ig_zsend, ig_zland, iz_s, iz_r, anti_dev)
    rows_first(1)
    ig_own[...] = ig_sum(1, tp)
    rows_last(2)
    rows_first(0)
    rows_last(1)
    rows_last(0)
    iz.wait_recv()
    ig_out[...] = unpack((ig_own[...] + ig_zland[...].astype(F32)).astype(BF16))

    for cp in sent:
        cp.wait_send()


def adam(ig, grad, master, mom_one, mom_two, ig_out, master_out, one_out, two_out):
    ig_out[...] = ig[...]
    one = beta_one * mom_one[...] + (1.0 - beta_one) * grad[...]
    two = beta_two * mom_two[...] + (1.0 - beta_two) * grad[...] * grad[...]
    update = one / bias_one / (jnp.sqrt(two / bias_two) + adam_eps) + decay_rate * master[...]
    master_out[...] = master[...] - learn_rate * update
    one_out[...] = one
    two_out[...] = two


def per_device(tokens, cotangent, working, degraded, block_map, master, moment_one, moment_two):
    vmem = pl.BlockSpec(memory_space=pltpu.VMEM)
    smem = pl.BlockSpec(memory_space=pltpu.SMEM)
    hbm = pl.BlockSpec(memory_space=pltpu.HBM)
    dma = pltpu.SemaphoreType.DMA
    rows = jax.ShapeDtypeStruct((3, 8, D), F32)
    shard = jax.ShapeDtypeStruct((TOK, SHARD), BF16)
    whole = pl.BlockSpec((TOK, SHARD), lambda k: (0, 0))
    third = pl.BlockSpec((1, 8, D), lambda k: (k, 0, 0))
    ig, grad = pl.pallas_call(
        kernel,
        name="swiglu_step",
        out_shape=(shard, rows),
        in_specs=[hbm, hbm, hbm, smem, smem],
        out_specs=(vmem, vmem),
        scratch_shapes=[
            pltpu.VMEM((3, SLOTS * BLOCK, D), BF16),
            pltpu.VMEM((2, TOK, SHARD), BF16),
            pltpu.VMEM((N_TP, 2, PACKED, BLOCK), BF16),
            pltpu.VMEM((GROUP, 2, PACKED, BLOCK), BF16),
            pltpu.VMEM((TOK, D), BF16),
            pltpu.VMEM((TOK, D), BF16),
            pltpu.SMEM((BLOCKS,), jnp.int32),
            pltpu.SMEM((SLOTS,), F32),
            pltpu.VMEM((N_Y, 3, UNIT, BLOCK), BF16),
            pltpu.VMEM((3, 2, TOK, BLOCK), BF16),
            pltpu.VMEM((3, 2, TOK, BLOCK), BF16),
            pltpu.VMEM((3, 2, TOK, BLOCK), BF16),
            pltpu.VMEM((GROUP, 3, 3 * BLOCK, BLOCK), BF16),
            pltpu.VMEM((N_TP, PACKED, BLOCK), BF16),
            pltpu.VMEM((3, 2, PACKED, BLOCK), BF16),
            pltpu.VMEM((PACKED, BLOCK), BF16),
            pltpu.VMEM((PACKED, BLOCK), BF16),
            pltpu.VMEM((PACKED, BLOCK), F32),
            pltpu.VMEM((2, TOK, SLOTS * BLOCK), F32),
            pltpu.VMEM((3, N_ZL, Z_ROWS, SHARD), F32),
            pltpu.VMEM((3, N_ZL, Z_PACKED, BLOCK), BF16),
            pltpu.VMEM((3, 3, Z_PACKED, BLOCK), BF16),
            pltpu.VMEM((3, GROUP, 8, SHARD), F32),
            pltpu.VMEM((3, GROUP, 8, SHARD), F32),
            dma((5,)),
            dma((2, 9)),
            dma((2, 9)),
            dma((7, 2)),
            dma((GROUP, 2)),
            dma((3, 4)),
            dma((3, 4)),
            dma((3,)),
            dma((3,)),
            dma((3, 8)),
            dma((3, 8)),
            dma((3, 2)),
            dma((3, 2)),
            dma,
            dma,
            dma((3, 3)),
            dma((3, 3)),
            dma((3, GROUP - 1)),
            dma((3, GROUP - 1)),
        ],
        compiler_params=pltpu.CompilerParams(
            collective_id=0, has_side_effects=True, vmem_limit_bytes=55 * 1024 * 1024
        ),
        cost_estimate=pl.CostEstimate(flops=3_700_000_000, bytes_accessed=12_000_000, transcendentals=73728),
    )(tokens, cotangent, working.reshape(working.shape[2:]), degraded, block_map)
    return pl.pallas_call(
        adam,
        name="adamw",
        out_shape=(shard, rows, rows, rows),
        grid=(3,),
        in_specs=[whole] + [third] * 4,
        out_specs=(whole,) + (third,) * 3,
        compiler_params=pltpu.CompilerParams(vmem_limit_bytes=55 * 1024 * 1024),
    )(ig, grad, master, moment_one, moment_two)


def solution(mesh):
    return jax.shard_map(
        per_device,
        mesh=mesh,
        in_specs=(
            P("dp", "tp"),
            P("dp", "tp"),
            P("dp", "tp", None, None, None),
            P("dp"),
            P("dp", None),
            P(None, ("tp", "dp"), None),
            P(None, ("tp", "dp"), None),
            P(None, ("tp", "dp"), None),
        ),
        out_specs=(
            P("dp", "tp"),
            P(None, ("tp", "dp"), None),
            P(None, ("tp", "dp"), None),
            P(None, ("tp", "dp"), None),
        ),
        check_vma=False,
    )
```
